512 devices in a mesh: tm: 64 (over z, x, core), space: 8 (over y).
Axes of the slice: x: 4, y: 8, z: 8, core: 2. Of those that a mesh axis runs over, the one named last changes fastest.
Arguments:
- nodes: float32 [64, 2, 2, 32, 128, 128], P('tm', None, None, 'space'), may hold values from -3 to 3
- initial: float32 [2, 32, 128, 128], P(None, 'space'), may hold values from -3 to 3
Outputs:
- corrected: float32 [64, 2, 2, 32, 128, 128], P('tm', None, None, 'space')
The draws below stay inside these ranges and needn't reach their ends.
All inputs are finite; a program needn't handle non-finite values.
Results may differ from the reference program's by a relative error of at most 0.0003.
Values sent between devices are 32-bit elements; how exact they have to be, the bound alone decides.
A program may use at most 128 MiB of HBM per device.

```python
import math
import jax
import jax.numpy as jnp
from jax import lax

NX = 128
NY = 128
SLICES = 64
NZ = 32


def level_of(rng, shape, shards, least, largest):
    loudness = 1.0
    for dim, parts in shards:
        heights = jax.random.uniform(jax.random.fold_in(jax.random.fold_in(rng, 6), dim), (parts,), jnp.float32, least / len(shards), largest / len(shards))
        loudness = loudness * jnp.repeat(jnp.exp(heights), shape[dim] // parts).reshape((-1,) + (1,) * (len(shape) - 1 - dim))
    return loudness


def centred(key, dims, deviation, most, pieces=(), dtype=jnp.bfloat16):
    result = deviation * jax.random.normal(key, dims, jnp.float32)
    if pieces:
        result = result * level_of(key, dims, pieces, -0.22, 0.18)
    return jnp.clip(result, -most, most).astype(dtype)


def setup_inputs(seed: int = 0) -> dict:
    streams_of = jax.random.split(jax.random.key(seed), 3)
    return {
        "nodes": centred(streams_of[0], (SLICES, 2, 2, NZ, NX, NY), 0.5, 3.0, ((0, 64), (3, 8)), jnp.float32),
        "initial": centred(streams_of[1], (2, NZ, NX, NY), 0.5, 3.0, ((1, 8),), jnp.float32),
    }


diffuse_fast = 0.5
diffuse_slow = 0.25
feed_rate = 0.04
kill_rate = 0.06
slice_length = 0.5
node_step = 0.25
sweep_weights = ((5.0 / 24.0, 1.0 / 3.0, -1.0 / 24.0), (-1.0 / 24.0, 1.0 / 3.0, 5.0 / 24.0))

def sine_table(points, modes, stretch):
    place = jnp.arange(points).astype(jnp.float32) + 0.5
    order = jnp.arange(modes).astype(jnp.float32) + 1.0
    angle = math.pi / (stretch * modes) * place[:, None] * order[None, :]
    weight = jnp.where(jnp.arange(modes) == modes - 1, math.sqrt(0.5), 1.0).astype(jnp.float32)
    return math.sqrt(2.0 / modes) * weight[None, :] * jnp.sin(angle)

def eigenvalues(count):
    order = jnp.arange(count).astype(jnp.float32) + 1.0
    return 2.0 * jnp.cos(math.pi * order / count) - 2.0

def tendency(values):
    center = values[..., 1:-1, :, :]
    padded = jnp.pad(center, [(0, 0)] * (center.ndim - 2) + [(1, 1), (1, 1)])
    laplace = values[..., 2:, :, :] + values[..., :-2, :, :] + padded[..., 2:, 1:-1] + padded[..., :-2, 1:-1]
    laplace = laplace + padded[..., 1:-1, 2:] + padded[..., 1:-1, :-2] - 6.0 * center
    first_kind = center[..., 0, :, :, :]
    second_kind = center[..., 1, :, :, :]
    reaction = (1.0 + first_kind) * second_kind * second_kind
    first_rate = diffuse_fast * laplace[..., 0, :, :, :] - reaction - feed_rate * first_kind
    second_rate = diffuse_slow * laplace[..., 1, :, :, :] + reaction - (feed_rate + kill_rate) * second_kind
    return jnp.stack([first_rate, second_rate], axis=-4)

def restrict(values):
    shape = values.shape
    blocks = values.reshape(shape[:-3] + (shape[-3] // 2, 2, shape[-2] // 2, 2, shape[-1] // 2, 2))
    return lax.optimization_barrier(jnp.mean(blocks, axis=(-5, -3, -1)))

def reference(nodes, initial):
    modes_x = NX // 2
    modes_y = NY // 2
    modes_z = NZ // 2
    forward_x = sine_table(modes_x, modes_x, 1.0).T
    forward_y = sine_table(modes_y, modes_y, 1.0).T
    forward_z = sine_table(modes_z, modes_z, 1.0).T
    interp_x = sine_table(NX, modes_x, 2.0)
    interp_y = sine_table(NY, modes_y, 2.0)
    interp_z = sine_table(NZ, modes_z, 2.0)
    eigen_sum = (eigenvalues(modes_z)[:, None, None] + eigenvalues(modes_x)[None, :, None] + eigenvalues(modes_y)[None, None, :]) / 4.0
    linear = jnp.stack([diffuse_fast * eigen_sum - feed_rate, diffuse_slow * eigen_sum - (feed_rate + kill_rate)])
    factor = 1.0 / (1.0 - node_step * linear)
    highest = lax.Precision.HIGHEST

    def widen(values):
        return jnp.pad(values, ((0, 0), (1, 1), (0, 0), (0, 0)))

    def forward(values):
        step_y = jnp.einsum('by,szxy->szxb', forward_y, values, precision=highest)
        step_x = jnp.einsum('ax,szxb->szab', forward_x, step_y, precision=highest)
        return jnp.einsum('kz,szab->skab', forward_z, step_x, precision=highest)

    def backward(spectra):
        step_z = jnp.einsum('zk,skab->szab', interp_z, spectra, precision=highest)
        step_y = jnp.einsum('yb,szab->szay', interp_y, step_z, precision=highest)
        return jnp.einsum('xa,szay->szxy', interp_x, step_y, precision=highest)
    (w00, w01, w02), (w10, w11, w12) = sweep_weights

    def advance(carry, inputs):
        prior_end, chain = carry
        own_nodes, position = inputs
        start_value = jnp.where(position == 0, initial, prior_end)
        middle = own_nodes[0]
        finish = own_nodes[1]
        slope_zero = tendency(widen(start_value))
        slope_mid = tendency(widen(middle))
        slope_end = tendency(widen(finish))
        swept_one = start_value + slice_length * (w00 * slope_zero + w01 * slope_mid + w02 * slope_end)
        slope_one = tendency(widen(swept_one))
        swept_two = swept_one + node_step * (slope_one - slope_mid) + slice_length * (w10 * slope_zero + w11 * slope_mid + w12 * slope_end)
        slope_two = tendency(widen(swept_two))
        integral_one = slice_length * (w00 * slope_zero + w01 * slope_one + w02 * slope_two)
        integral_two = slice_length * (w10 * slope_zero + w11 * slope_one + w12 * slope_two)
        quad_one = forward(restrict(integral_one))
        quad_two = forward(restrict(integral_two))
        coarse_zero = forward(restrict(start_value))
        coarse_one = forward(restrict(swept_one))
        coarse_two = forward(restrict(swept_two))
        remain_one = quad_one - node_step * linear * coarse_one
        remain_two = quad_two - node_step * linear * coarse_two
        start_hat = jnp.where(position == 0, coarse_zero, chain)
        new_one = factor * (start_hat + remain_one)
        new_two = factor * (new_one + remain_two)
        out_one = swept_one + backward(new_one - coarse_one)
        out_two = swept_two + backward(new_two - coarse_two)
        return ((finish, new_two), jnp.stack([out_one, out_two]))
    empty = jnp.zeros((2, modes_z, modes_x, modes_y), jnp.float32)
    positions = jnp.arange(SLICES).astype(jnp.int32)
    _, corrected = lax.scan(advance, (initial, empty), (nodes, positions))
    return corrected
```

```python
import functools
import math

import jax
import jax.numpy as jnp
import ml_dtypes
import numpy as np
from jax import lax
from jax.experimental import pallas as pl
from jax.experimental.pallas import tpu as pltpu
from jax.sharding import PartitionSpec as P

MESH = pl.DeviceIdType.MESH
DIFFUSE = (0.5, 0.25)
DECAY = (0.04, 0.1)
SIGN = (-1.0, 1.0)
DT = 0.5
H = 0.25
S = ((5.0 / 24.0, 1.0 / 3.0, -1.0 / 24.0), (-1.0 / 24.0, 1.0 / 3.0, 5.0 / 24.0))
ROWS = 32


def sine_table(points, modes, stretch):
    place = np.arange(points) + 0.5
    order = np.arange(modes) + 1.0
    angle = math.pi / (stretch * modes) * place[:, None] * order[None, :]
    weight = np.where(np.arange(modes) == modes - 1, math.sqrt(0.5), 1.0)
    return math.sqrt(2.0 / modes) * weight[None, :] * np.sin(angle)


def two_parts(table):
    high = table.astype(np.float32).astype(ml_dtypes.bfloat16)
    low = (table - high.astype(np.float64)).astype(np.float32).astype(ml_dtypes.bfloat16)
    return np.stack([high, low])


@functools.lru_cache(maxsize=None)
def tables(n, spaces):
    m, mz = n // 2, 2 * spaces
    half = m // 2
    per = half // spaces
    average = np.kron(np.eye(m), np.array([[0.5, 0.5]]))
    fine = sine_table(m, m, 1.0).T @ average
    fx = np.zeros((2, half, 2, 2, n))
    for z in range(2):
        fx[:, :, z, z, :] = 0.5 * fine.reshape(2, half, n)
    fx = fx.reshape(2 * m, 2 * n)
    fy = np.kron(np.eye(2), fine.T)
    wz = sine_table(mz, mz, 1.0).T
    own = np.zeros((mz, per, spaces, per, 2))
    edge = np.zeros((mz, per, spaces, per, 2))
    for i in range(per):
        for y in range(spaces):
            for z in range(2):
                own[:, i, y, i, z] = wz[:, 2 * y + z]
            if y > 0:
                edge[:, i, y, i, 0] = wz[:, 2 * y - 1]
            if y < spaces - 1:
                edge[:, i, y, i, 1] = wz[:, 2 * y + 2]
    own, edge = own.reshape(m, m), edge.reshape(m, m)
    mats = np.stack(
        [np.concatenate([own, edge * (DT * S[i][2])], axis=1) for i in range(2)]
    )
    nz = np.kron(sine_table(2 * mz, mz, 2.0), np.eye(per))
    vxy = sine_table(n, m, 2.0)
    vy = np.kron(np.eye(2), vxy.T)
    vx = np.zeros((4, n, 2, spaces, 4, per))
    for f in range(4):
        vx[f, :, :, :, f, :] = vxy.reshape(n, 2, spaces, per)
    vx = vx.reshape(4 * n, 2 * spaces * 4 * per)

    def eigen(modes):
        return 2.0 * np.cos(math.pi * (np.arange(modes) + 1.0) / modes) - 2.0

    ab = (eigen(m)[:, None] + eigen(m)[None, :]).reshape(2, spaces, per, m)
    e = (eigen(mz)[None, :, None, None, None] + ab.transpose(1, 2, 0, 3)[:, None]) / 4.0
    lin = np.stack([d * e - k for d, k in zip(DIFFUSE, DECAY)])
    factor = 1.0 / (1.0 - H * lin)
    factor = factor.reshape(2, spaces, m, n).astype(np.float32)
    return tuple(map(two_parts, (fx, fy, mats[0], mats[1], nz, vy, vx))) + (factor,)


def split(x):
    high = x.astype(jnp.bfloat16)
    low = (x - high.astype(jnp.float32)).astype(jnp.bfloat16)
    return high, low


def dot(a, b):
    return jnp.dot(a, b, preferred_element_type=jnp.float32)


def left(table, x):
    high, low = split(x)
    return dot(table[0], high) + (dot(table[0], low) + dot(table[1], high))


def right(x, table):
    high, low = split(x)
    return dot(high, table[0]) + (dot(low, table[0]) + dot(high, table[1]))


def kernel(
    shape,
    nodes, initial, fx_h, fy_h, m0_h, m1_h, nz_h, vy_h, vx_h, p_h,
    out,
    u, s1, s2, a, g, fx, fy, m0, m1, nz, vy, vx, pw,
    spec, c2in, gather, e2, xin, tot, zin, back, pre, fine, fin,
    ssem, lsem, r_u0, r_h, r_u0h, r_s1, r_c2, r_in, r_x, r_z, r_b, r_f,
):
    count, spaces, chips_x, chips_z, n = shape
    tm, sp = lax.axis_index("tm"), lax.axis_index("space")
    core = lax.rem(tm, 2)
    chip = tm // 2
    cx, cz = lax.rem(chip, chips_x), chip // chips_x
    sends = []

    def at(z, x, c):
        return (z * chips_x + x) * 2 + c

    def send(src, dst, sem, device, when=None):
        copy = pltpu.make_async_remote_copy(
            src, dst, ssem.at[len(sends)], sem, device_id=device, device_id_type=MESH
        )
        sends.append((copy, when))
        if when is None:
            copy.start()
        else:
            pl.when(when)(copy.start)

    def arrived(dst, sem):
        pltpu.make_async_copy(dst, dst, sem).wait()

    has_lo, has_hi = sp > 0, sp < spaces - 1
    lo, hi = (tm, jnp.maximum(sp - 1, 0)), (tm, jnp.minimum(sp + 1, spaces - 1))
    has_next, has_prior = tm < count - 1, tm > 0
    nxt = (lax.rem(tm + 1, count), sp)
    prv = (lax.rem(tm + count - 1, count), sp)
    yc = [(d % spaces, d // spaces) for d in range(1, 2 * spaces)]

    def owner(d):
        return lax.rem(sp + d[0], spaces), lax.rem(core + d[1], 2)

    x_peers = [lax.rem(cx + d, chips_x) for d in range(1, chips_x)]
    z_peers = [lax.rem(cz + d, chips_z) for d in range(1, chips_z)]

    loads = [
        pltpu.make_async_copy(nodes.at[0, 0], u.at[1, :, pl.ds(1, 4)], lsem.at[0]),
        pltpu.make_async_copy(nodes.at[0, 1], u.at[2, :, pl.ds(1, 4)], lsem.at[1]),
        pltpu.make_async_copy(fx_h, fx, lsem.at[2]),
        pltpu.make_async_copy(fy_h, fy, lsem.at[3]),
        pltpu.make_async_copy(m0_h, m0, lsem.at[4]),
        pltpu.make_async_copy(m1_h, m1, lsem.at[5]),
        pltpu.make_async_copy(nz_h, nz, lsem.at[6]),
        pltpu.make_async_copy(vy_h, vy, lsem.at[7]),
        pltpu.make_async_copy(vx_h, vx, lsem.at[8]),
        pltpu.make_async_copy(p_h.at[core, sp], pw, lsem.at[9]),
    ]
    for load in loads:
        load.start()
    pieces = [(0, 1), (3, 1), (1, 2)]

    @pl.when(tm == 0)
    def _():
        for i, (z, length) in enumerate(pieces):
            pltpu.make_async_copy(
                initial.at[:, pl.ds(z, length)], u.at[0, :, pl.ds(1 + z, length)], r_u0.at[i]
            ).start()

    barrier = pltpu.get_barrier_semaphore()
    peers = []
    for d in yc:
        y, c = owner(d)
        peers.append((chip * 2 + c, y))
    peers += [(at(cz, x, core), sp) for x in x_peers]
    peers += [(at(z, cx, core), sp) for z in z_peers]
    peers.append((lax.rem(tm + count - 1 + 2 * core, count), sp))
    for peer in peers:
        pl.semaphore_signal(barrier, 1, device_id=peer, device_id_type=MESH)
    pl.semaphore_wait(barrier, len(peers))

    for node in (2, 1):
        send(nodes.at[0, node - 1, :, 3], u.at[node, :, 0], r_h.at[node - 1, 0], hi, has_hi)
        send(nodes.at[0, node - 1, :, 0], u.at[node, :, 5], r_h.at[node - 1, 1], lo, has_lo)
    for i, (z, length) in enumerate(pieces):
        send(
            nodes.at[0, 1, :, pl.ds(z, length)], u.at[0, :, pl.ds(1 + z, length)],
            r_u0.at[i], nxt, has_next,
        )

    zero = jnp.zeros((n, n), jnp.float32)
    for s in range(2):
        for z in range(6):
            a[s, z, 0:8, :] = jnp.zeros((8, n), jnp.float32)
            a[s, z, 8 + n : 16 + n, :] = jnp.zeros((8, n), jnp.float32)

    def outside(plane):
        for s in range(2):
            for i in range(3):
                u[i, s, plane] = zero
            s1[s, plane] = zero

    pl.when(sp == 0)(lambda: outside(0))
    pl.when(sp == spaces - 1)(lambda: outside(5))

    @pl.when(tm == 0)
    def _():
        c2in[...] = jnp.zeros(c2in.shape, jnp.float32)

    lane = lax.broadcasted_iota(jnp.int32, (ROWS, n), 1)
    first_lane, last_lane = lane == 0, lane == n - 1
    chunks = range(0, n, ROWS)

    def react(p, q):
        return (1.0 + p) * (q * q)

    def sides(s, z, r):
        mid = a[s, z, 8 + r : 8 + r + ROWS, :]
        west = jnp.where(first_lane, 0.0, pltpu.roll(mid, 1, 1))
        east = jnp.where(last_lane, 0.0, pltpu.roll(mid, n - 1, 1))
        north = a[s, z, 7 + r : 7 + r + ROWS, :]
        south = a[s, z, 9 + r : 9 + r + ROWS, :]
        return (west + east) + (north + south), mid

    def rows(ref, *index, r):
        return ref[(*index, slice(r, r + ROWS), slice(None))]

    def sum_one(z, base=True):
        for r in chunks:
            pq = [[rows(u, i, s, z, r=r) for s in range(2)] for i in range(3)]
            if base:
                w = sum((DT * S[0][i]) * react(*pq[i]) for i in range(3))
            for s in range(2):
                total = sum((DT * S[0][i]) * pq[i][s] for i in range(3))
                a[s, z, 8 + r : 8 + r + ROWS, :] = total
                if base:
                    s1[s, z, r : r + ROWS, :] = pq[0][s] + SIGN[s] * w - DECAY[s] * total

    def sum_two(z, base=True):
        weight = (DT * S[1][0], DT * S[1][1] - H, DT * S[1][2])
        for r in chunks:
            pq = [[rows(u, i, s, z, r=r) for s in range(2)] for i in range(3)]
            ab = [rows(s1, s, z, r=r) for s in range(2)]
            if base:
                w = H * react(*ab) + sum(weight[i] * react(*pq[i]) for i in range(3))
            for s in range(2):
                total = H * ab[s] + sum(weight[i] * pq[i][s] for i in range(3))
                a[s, z, 8 + r : 8 + r + ROWS, :] = total
                if base:
                    s2[s, z - 1, r : r + ROWS, :] = ab[s] + SIGN[s] * w - DECAY[s] * total

    def diffuse(ref, z, shift):
        for r in chunks:
            for s in range(2):
                around, mid = sides(s, z, r)
                below = a[s, z - 1, 8 + r : 8 + r + ROWS, :]
                above = a[s, z + 1, 8 + r : 8 + r + ROWS, :]
                lap = around + (below + above) - 6.0 * mid
                ref[s, z - shift, r : r + ROWS, :] = (
                    ref[s, z - shift, r : r + ROWS, :] + DIFFUSE[s] * lap
                )

    loads[0].wait()
    loads[1].wait()
    even = core == 0
    arrived(u.at[0, :, pl.ds(1, 1)], r_u0.at[0])
    arrived(u.at[0, :, pl.ds(4, 1)], r_u0.at[1])
    send(u.at[0, :, 4], u.at[0, :, 0], r_u0h.at[0], hi, has_hi & even)
    send(u.at[0, :, 1], u.at[0, :, 5], r_u0h.at[1], lo, has_lo & even)
    pl.when(has_lo)(lambda: arrived(u.at[2, :, 0], r_h.at[1, 0]))
    pl.when(has_hi)(lambda: arrived(u.at[2, :, 5], r_h.at[1, 1]))
    send(u.at[2, :, 0], u.at[0, :, 0], r_u0h.at[0], nxt, has_lo & even)
    send(u.at[2, :, 5], u.at[0, :, 5], r_u0h.at[1], nxt, has_hi & even)
    arrived(u.at[0, :, pl.ds(2, 2)], r_u0.at[2])
    for z in (1, 2, 3, 4):
        sum_one(z)
    for z in (2, 3):
        diffuse(s1, z, 0)
    pl.when(has_lo)(lambda: arrived(u.at[1, :, 0], r_h.at[0, 0]))
    pl.when(has_lo)(lambda: arrived(u.at[0, :, 0], r_u0h.at[0]))
    sum_one(0, False)
    diffuse(s1, 1, 0)
    send(s1.at[:, 1], s1.at[:, 5], r_s1.at[1], lo, has_lo)
    pl.when(has_hi)(lambda: arrived(u.at[1, :, 5], r_h.at[0, 1]))
    pl.when(has_hi)(lambda: arrived(u.at[0, :, 5], r_u0h.at[1]))
    sum_one(5, False)
    diffuse(s1, 4, 0)
    send(s1.at[:, 4], s1.at[:, 0], r_s1.at[0], hi, has_hi)

    for z in (1, 2, 3, 4):
        sum_two(z)
    for z in (2, 3):
        diffuse(s2, z, 1)
    pl.when(has_lo)(lambda: arrived(s1.at[:, 0], r_s1.at[0]))
    pl.when(has_hi)(lambda: arrived(s1.at[:, 5], r_s1.at[1]))
    sum_two(0, False)
    sum_two(5, False)
    diffuse(s2, 1, 1)
    diffuse(s2, 4, 1)

    is_first = jnp.where(tm == 0, 1.0, 0.0)
    for i in range(2):
        for j in range(2):
            z = 2 * j + 1
            for r in chunks:
                w = 0.0
                both = [0.0, 0.0]
                keep = [0.0, 0.0]
                for k in (z, z + 1):
                    p0 = [rows(u, 0, s, k, r=r) for s in range(2)]
                    p1 = [rows(s1, s, k, r=r) for s in range(2)]
                    p2 = [rows(s2, s, k - 1, r=r) for s in range(2)]
                    three = (p0, p1, p2)
                    w = w + sum((DT * S[i][t]) * react(*three[t]) for t in range(3))
                    for s in range(2):
                        total = sum((DT * S[i][t]) * three[t][s] for t in range(3))
                        both[s] = both[s] + total
                        if i == 0:
                            keep[s] = keep[s] + is_first * p0[s] - p1[s]
                        else:
                            keep[s] = keep[s] + p1[s] - p2[s]
                for s in range(2):
                    out_of = 0 if j == 0 else 5
                    near = 3 if j == 0 else 2
                    beyond = (DT * S[i][0]) * rows(u, 0, s, out_of, r=r) + (DT * S[i][1]) * rows(
                        s1, s, out_of, r=r
                    )
                    beyond = beyond + (
                        (DT * S[i][0]) * rows(u, 0, s, near, r=r)
                        + (DT * S[i][1]) * rows(s1, s, near, r=r)
                        + (DT * S[i][2]) * rows(s2, s, near - 1, r=r)
                    )
                    a[s, j, 8 + r : 8 + r + ROWS, :] = both[s]
                    g[i, j, r : r + ROWS, s * n : (s + 1) * n] = (
                        keep[s]
                        + SIGN[s] * w
                        - DECAY[s] * both[s]
                        + DIFFUSE[s] * (beyond - 5.0 * both[s])
                    )
            for r in chunks:
                for s in range(2):
                    around, _ = sides(s, j, r)
                    at_s = slice(s * n, (s + 1) * n)
                    g[i, j, r : r + ROWS, at_s] = (
                        g[i, j, r : r + ROWS, at_s] + DIFFUSE[s] * around
                    )
    for j in range(2):
        for r in chunks:
            for s in range(2):
                at_s = slice(s * n, (s + 1) * n)
                g[2, j, r : r + ROWS, at_s] = DIFFUSE[s] * rows(s2, s, 3 * j, r=r)
                g[3, j, r : r + ROWS, at_s] = rows(s2, s, 2 * j, r=r) + rows(s2, s, 2 * j + 1, r=r)

    for load in loads[2:]:
        load.wait()

    def to_modes(i):
        both = jnp.concatenate([g[i, 0], g[i, 1]], axis=0)
        along_x = left(fx, both)
        for s in range(2):
            at_s = slice(s * n, (s + 1) * n)
            wide = jnp.concatenate([along_x[: n // 2, at_s], along_x[n // 2 :, at_s]], axis=1)
            spec[s, i] = right(wide, fy)

    part = n // 2 // spaces
    to_modes(3)
    send(spec.at[:, 3], c2in, r_c2, nxt, has_next)
    for i in (1, 2, 0):
        to_modes(i)
    pl.when(has_prior)(lambda: arrived(c2in, r_c2))
    for s in range(2):
        spec[s, 0] = spec[s, 0] + c2in[s]

    def mine(y):
        return pl.ds(pl.multiple_of(y * part, part), part)

    for d in yc:
        y, c = owner(d)
        send(spec.at[c, pl.ds(0, 3), mine(y)], gather.at[core, :, sp], r_in.at[core, sp], (chip * 2 + c, y))
    gather[core, :, sp] = spec[core, 0:3, mine(sp)]
    for d in yc:
        y, c = owner(d)
        arrived(gather.at[c, :, y], r_in.at[c, y])

    m = n // 2
    power = pw[...]
    square = power * power
    d0, d1 = [], []
    for c in range(2):
        own = [gather[c, i].reshape(m, n) for i in range(3)]
        d0.append(left(m0, jnp.concatenate([own[0], own[2]], axis=0)))
        d1.append(left(m1, jnp.concatenate([own[1], own[2]], axis=0)))
    e = [power * (power * d0[c] + d1[c]) for c in range(2)]
    e2[...] = square * e[0] + e[1]

    share = m // chips_x

    def shared(x):
        return pl.ds(pl.multiple_of(x * share, share), share)

    for x in x_peers:
        send(e2.at[shared(x)], xin.at[cx], r_x.at[cx], (at(cz, x, core), sp))
    xin[cx] = e2[shared(cx)]
    for x in x_peers:
        arrived(xin.at[x], r_x.at[x])
    p1 = pw[shared(cx)]
    p2 = p1 * p1
    p4 = p2 * p2
    running = jnp.zeros((share, n), jnp.float32)
    before, ahead = [], []
    power_x = jnp.ones((share, n), jnp.float32)
    for x in range(chips_x):
        before.append(running)
        ahead.append(power_x)
        running = p4 * running + xin[x]
        power_x = power_x * p4
    tot[...] = running
    for z in z_peers:
        send(tot, zin.at[cz], r_z.at[cz], (at(z, cx, core), sp))
    zin[cz] = running
    for z in z_peers:
        arrived(zin.at[z], r_z.at[z])
    earlier = jnp.zeros((share, n), jnp.float32)
    for z in range(chips_z):
        earlier = jnp.where(z < cz, power_x * earlier + zin[z], earlier)
    for x in range(chips_x):
        back[x] = ahead[x] * earlier + before[x]
    for x in x_peers:
        send(back.at[x], pre.at[shared(cx)], r_b.at[cx], (at(cz, x, core), sp))
    pre[shared(cx)] = back[cx]
    for x in x_peers:
        arrived(pre.at[shared(x)], r_b.at[x])

    change = pre[...]
    for c in range(2):
        for f, source in enumerate((d0[c], d1[c])):
            change = power * (change + source)
            fine[c, f] = left(nz, change)
    rows_back = 2 * part

    def planes(y):
        return pl.ds(pl.multiple_of(y * rows_back, rows_back), rows_back)

    for d in yc:
        y, c = owner(d)
        send(fine.at[c, :, planes(y)], fin.at[:, core, sp], r_f.at[core, sp], (chip * 2 + c, y))
    fin[:, core, sp] = fine[core, :, planes(sp)]
    for d in yc:
        y, c = owner(d)
        arrived(fin.at[:, c, y], r_f.at[c, y])

    for f in range(2):
        tall = []
        for s in range(2):
            wide = right(fin[f, s].reshape(n, n), vy)
            tall.append(jnp.concatenate([wide[:, :n], wide[:, n:]], axis=0))
        refined = left(vx, jnp.concatenate(tall, axis=1))
        for s in range(2):
            for z in range(4):
                piece = refined[z * n : (z + 1) * n, s * n : (s + 1) * n]
                swept = s1[s, z + 1] if f == 0 else s2[s, z]
                out[0, f, s, z] = swept + piece

    for copy, when in sends:
        if when is None:
            copy.wait_send()
        else:
            pl.when(when)(copy.wait_send)


def local(shape, nodes, initial):
    count, spaces, chips_x, chips_z, n = shape
    consts = tables(n, spaces)
    m = n // 2
    part = m // spaces
    share = m // chips_x
    f32 = jnp.float32
    vmem, sem = pltpu.VMEM, pltpu.SemaphoreType.DMA
    n_sends = 4 + 3 + 4 + 2 + 1 + 2 * (2 * spaces - 1) + 2 * (chips_x - 1) + chips_z - 1
    scratch = [
        vmem((3, 2, 6, n, n), f32),
        vmem((2, 6, n, n), f32),
        vmem((2, 4, n, n), f32),
        vmem((2, 6, n + 16, n), f32),
        vmem((4, 2, n, 2 * n), f32),
    ]
    scratch += [vmem(c.shape, jnp.bfloat16) for c in consts[:-1]]
    scratch += [
        vmem((m, n), f32),
        vmem((2, 4, m, n), f32),
        vmem((2, m, n), f32),
        vmem((2, 3, spaces, part, n), f32),
        vmem((m, n), f32),
        vmem((chips_x, share, n), f32),
        vmem((share, n), f32),
        vmem((chips_z, share, n), f32),
        vmem((chips_x, share, n), f32),
        vmem((m, n), f32),
        vmem((2, 2, n, n), f32),
        vmem((2, 2, spaces, 2 * part, n), f32),
        sem((n_sends,)),
        sem((10,)),
        sem((3,)),
        sem((2, 2)),
        sem((2,)),
        sem((2,)),
        sem(()),
        sem((2, spaces)),
        sem((chips_x,)),
        sem((chips_z,)),
        sem((chips_x,)),
        sem((2, spaces)),
    ]
    anywhere = pl.BlockSpec(memory_space=pl.ANY)
    return pl.pallas_call(
        functools.partial(kernel, shape),
        out_shape=jax.ShapeDtypeStruct((1, 2, 2, 4, n, n), f32),
        in_specs=[anywhere] * (2 + len(consts)),
        out_specs=pl.BlockSpec(memory_space=pltpu.VMEM),
        scratch_shapes=scratch,
        compiler_params=pltpu.CompilerParams(
            collective_id=0, has_side_effects=True, vmem_limit_bytes=48 << 20
        ),
        name="iteration",
    )(nodes, initial, *[jnp.asarray(c) for c in consts])


def solution(mesh):
    count, spaces = mesh.shape["tm"], mesh.shape["space"]
    chips_x = 4 if count == 64 else 2
    chips_z = count // (2 * chips_x)
    in_specs = (P("tm", None, None, "space", None, None), P(None, "space", None, None))
    out_specs = P("tm", None, None, "space", None, None)

    def run(nodes, initial):
        shape = (count, spaces, chips_x, chips_z, nodes.shape[-1])
        return jax.shard_map(
            functools.partial(local, shape),
            mesh=mesh, in_specs=in_specs, out_specs=out_specs, check_vma=False,
        )(nodes, initial)

    return run
```

```python
import functools
import math

import jax
import jax.numpy as jnp
import ml_dtypes
import numpy as np
from jax import lax
from jax.experimental import pallas as pl
from jax.experimental.pallas import tpu as pltpu
from jax.sharding import PartitionSpec as P

MESH = pl.DeviceIdType.MESH
DIFFUSE = (0.5, 0.25)
DECAY = (0.04, 0.1)
SIGN = (-1.0, 1.0)
DT = 0.5
H = 0.25
S = ((5.0 / 24.0, 1.0 / 3.0, -1.0 / 24.0), (-1.0 / 24.0, 1.0 / 3.0, 5.0 / 24.0))
ROWS = 32


def sine_table(points, modes, stretch):
    place = np.arange(points) + 0.5
    order = np.arange(modes) + 1.0
    angle = math.pi / (stretch * modes) * place[:, None] * order[None, :]
    weight = np.where(np.arange(modes) == modes - 1, math.sqrt(0.5), 1.0)
    return math.sqrt(2.0 / modes) * weight[None, :] * np.sin(angle)


def two_parts(table):
    high = table.astype(np.float32).astype(ml_dtypes.bfloat16)
    low = (table - high.astype(np.float64)).astype(np.float32).astype(ml_dtypes.bfloat16)
    return np.stack([high, low])


@functools.lru_cache(maxsize=None)
def tables(n, spaces):
    m, mz = n // 2, 2 * spaces
    half = m // 2
    per = half // spaces
    average = np.kron(np.eye(m), np.array([[0.5, 0.5]]))
    fine = sine_table(m, m, 1.0).T @ average
    fx = np.zeros((2, half, 2, 2, n))
    for z in range(2):
        fx[:, :, z, z, :] = 0.5 * fine.reshape(2, half, n)
    fx = fx.reshape(2 * m, 2 * n)
    fy = np.kron(np.eye(2), fine.T)
    wz = sine_table(mz, mz, 1.0).T
    own = np.zeros((mz, per, spaces, per, 2))
    edge = np.zeros((mz, per, spaces, per, 2))
    for i in range(per):
        for y in range(spaces):
            for z in range(2):
                own[:, i, y, i, z] = wz[:, 2 * y + z]
            if y > 0:
                edge[:, i, y, i, 0] = wz[:, 2 * y - 1]
            if y < spaces - 1:
                edge[:, i, y, i, 1] = wz[:, 2 * y + 2]
    own, edge = own.reshape(m, m), edge.reshape(m, m)
    mats = np.stack(
        [np.concatenate([own, edge * (DT * S[i][2])], axis=1) for i in range(2)]
    )
    nz = np.kron(sine_table(2 * mz, mz, 2.0), np.eye(per))
    vxy = sine_table(n, m, 2.0)
    vy = np.kron(np.eye(2), vxy.T)
    vx = np.zeros((4, n, 2, spaces, 4, per))
    for f in range(4):
        vx[f, :, :, :, f, :] = vxy.reshape(n, 2, spaces, per)
    vx = vx.reshape(4 * n, 2 * spaces * 4 * per)

    def eigen(modes):
        return 2.0 * np.cos(math.pi * (np.arange(modes) + 1.0) / modes) - 2.0

    ab = (eigen(m)[:, None] + eigen(m)[None, :]).reshape(2, spaces, per, m)
    e = (eigen(mz)[None, :, None, None, None] + ab.transpose(1, 2, 0, 3)[:, None]) / 4.0
    lin = np.stack([d * e - k for d, k in zip(DIFFUSE, DECAY)])
    factor = 1.0 / (1.0 - H * lin)
    factor = factor.reshape(2, spaces, m, n).astype(np.float32)
    return tuple(map(two_parts, (fx, fy, mats[0], mats[1], nz, vy, vx))) + (factor,)


def split(x):
    high = x.astype(jnp.bfloat16)
    low = (x - high.astype(jnp.float32)).astype(jnp.bfloat16)
    return high, low


def dot(a, b):
    return jnp.dot(a, b, preferred_element_type=jnp.float32)


def left(table, x):
    high, low = split(x)
    return dot(table[0], high) + (dot(table[0], low) + dot(table[1], high))


def right(x, table):
    high, low = split(x)
    return dot(high, table[0]) + (dot(low, table[0]) + dot(high, table[1]))


def kernel(
    shape,
    nodes, initial, fx_h, fy_h, m0_h, m1_h, nz_h, vy_h, vx_h, p_h,
    out,
    u, s1, s2, a, g, fx, fy, m0, m1, nz, vy, vx, pw,
    spec, c2out, c2in, gather, e2, xin, tot, zin, back, pre, fine, fin,
    ssem, lsem, r_u0, r_h, r_u0h, r_s1, r_c2, r_in, r_x, r_z, r_b, r_f, credit,
):
    count, spaces, chips_x, chips_z, n = shape
    tm, sp = lax.axis_index("tm"), lax.axis_index("space")
    core = lax.rem(tm, 2)
    chip = tm // 2
    cx, cz = lax.rem(chip, chips_x), chip // chips_x
    sends = []

    def at(z, x, c):
        return (z * chips_x + x) * 2 + c

    def send(src, dst, sem, device, when=None):
        copy = pltpu.make_async_remote_copy(
            src, dst, ssem.at[len(sends)], sem, device_id=device, device_id_type=MESH
        )
        sends.append((copy, when))
        if when is None:
            copy.start()
        else:
            pl.when(when)(copy.start)

    def arrived(dst, sem):
        pltpu.make_async_copy(dst, dst, sem).wait()

    has_lo, has_hi = sp > 0, sp < spaces - 1
    lo, hi = (tm, jnp.maximum(sp - 1, 0)), (tm, jnp.minimum(sp + 1, spaces - 1))
    has_next, has_prior = tm < count - 1, tm > 0
    nxt = (lax.rem(tm + 1, count), sp)
    prv = (lax.rem(tm + count - 1, count), sp)
    ring = sorted(range(spaces), key=lambda d: -min(d, spaces - d))
    yc = [(d, c) for d in ring for c in (1, 0) if (d, c) != (0, 0)]

    def owner(d):
        return lax.rem(sp + d[0], spaces), lax.rem(core + d[1], 2)

    x_peers = [lax.rem(cx + d, chips_x) for d in (2, 1, 3) if d < chips_x]
    if chips_x == 2:
        x_peers = [1 - cx]

    loads = [
        pltpu.make_async_copy(nodes.at[0, 0], u.at[1, :, pl.ds(1, 4)], lsem.at[0]),
        pltpu.make_async_copy(nodes.at[0, 1], u.at[2, :, pl.ds(1, 4)], lsem.at[1]),
        pltpu.make_async_copy(fx_h, fx, lsem.at[2]),
        pltpu.make_async_copy(fy_h, fy, lsem.at[3]),
        pltpu.make_async_copy(m0_h, m0, lsem.at[4]),
        pltpu.make_async_copy(m1_h, m1, lsem.at[5]),
        pltpu.make_async_copy(nz_h, nz, lsem.at[6]),
        pltpu.make_async_copy(vy_h, vy, lsem.at[7]),
        pltpu.make_async_copy(vx_h, vx, lsem.at[8]),
        pltpu.make_async_copy(p_h.at[core, sp], pw, lsem.at[9]),
    ]
    for load in loads:
        load.start()
    pieces = [(0, 1), (3, 1), (1, 2)]

    @pl.when(tm == 0)
    def _():
        for i, (z, length) in enumerate(pieces):
            pltpu.make_async_copy(
                initial.at[:, pl.ds(z, length)], u.at[0, :, pl.ds(1 + z, length)], r_u0.at[i]
            ).start()

    barrier = pltpu.get_barrier_semaphore()
    sibling = tm + 1 - 2 * core
    crosses = jnp.where(core == 1, cx == chips_x - 1, cx == 0)
    beside = lax.rem(tm + count - 1 + 2 * core, count)
    has_beside = jnp.where(core == 1, has_next, has_prior)

    def greet(t, y):
        pl.semaphore_signal(barrier, 1, device_id=(t, y), device_id_type=MESH)

    def answer(which, t, y):
        pl.semaphore_signal(credit.at[which], 1, device_id=(t, y), device_id_type=MESH)

    def waits_for(which, answers):
        pl.when(answers > 0)(lambda: pl.semaphore_wait(credit.at[which], answers))

    def over(lower, upper, work):
        def step(i, carry):
            work(i)
            return carry

        lax.fori_loop(lower, upper, step, 0)

    def far_columns(y, call):
        call(sibling, y)
        pl.when((y != sp + 1) & (y != sp - 1))(lambda: call(tm, y))

    pl.when(has_hi)(lambda: greet(tm, hi[1]))
    pl.when(has_lo)(lambda: greet(tm, lo[1]))
    greet(sibling, sp)
    pl.when(has_beside & (~crosses | (core == 1)))(lambda: greet(beside, sp))
    over(sp + 1, spaces, lambda y: far_columns(y, greet))
    over(cx + 1, chips_x, lambda x: greet(at(cz, x, core), sp))
    over(cz + 1, chips_z, lambda z: greet(at(z, cx, core), sp))

    def one(flag):
        return jnp.where(flag, 1, 0)

    below_far = 2 * sp - one(has_lo)
    above_far = 2 * (spaces - 1 - sp) - one(has_hi)
    pl.semaphore_wait(
        barrier,
        one(has_lo) + one(has_hi) + 1 + one(has_beside & (~crosses | (core == 0)))
        + below_far + cx + cz,
    )
    pl.when(has_beside & crosses & (core == 0))(lambda: answer(3, beside, sp))

    for node in (2, 1):
        send(nodes.at[0, node - 1, :, 3], u.at[node, :, 0], r_h.at[node - 1, 0], hi, has_hi)
        send(nodes.at[0, node - 1, :, 0], u.at[node, :, 5], r_h.at[node - 1, 1], lo, has_lo)
    waits_for(3, one(has_beside & crosses & (core == 1)))
    for i, (z, length) in enumerate(pieces):
        send(
            nodes.at[0, 1, :, pl.ds(z, length)], u.at[0, :, pl.ds(1 + z, length)],
            r_u0.at[i], nxt, has_next,
        )

    over(0, sp, lambda y: far_columns(y, functools.partial(answer, 0)))
    over(0, cx, lambda x: answer(1, at(cz, x, core), sp))
    over(0, cz, lambda z: answer(2, at(z, cx, core), sp))

    zero = jnp.zeros((n, n), jnp.float32)
    for s in range(2):
        for z in range(6):
            a[s, z, 0:8, :] = jnp.zeros((8, n), jnp.float32)
            a[s, z, 8 + n : 16 + n, :] = jnp.zeros((8, n), jnp.float32)

    def outside(plane):
        for s in range(2):
            for i in range(3):
                u[i, s, plane] = zero
            s1[s, plane] = zero

    pl.when(sp == 0)(lambda: outside(0))
    pl.when(sp == spaces - 1)(lambda: outside(5))

    @pl.when(tm == 0)
    def _():
        c2in[...] = jnp.zeros(c2in.shape, jnp.float32)

    lane = lax.broadcasted_iota(jnp.int32, (ROWS, n), 1)
    first_lane, last_lane = lane == 0, lane == n - 1
    chunks = range(0, n, ROWS)

    def react(p, q):
        return (1.0 + p) * (q * q)

    def sides(s, z, r):
        mid = a[s, z, 8 + r : 8 + r + ROWS, :]
        west = jnp.where(first_lane, 0.0, pltpu.roll(mid, 1, 1))
        east = jnp.where(last_lane, 0.0, pltpu.roll(mid, n - 1, 1))
        north = a[s, z, 7 + r : 7 + r + ROWS, :]
        south = a[s, z, 9 + r : 9 + r + ROWS, :]
        return (west + east) + (north + south), mid

    def rows(ref, *index, r):
        return ref[(*index, slice(r, r + ROWS), slice(None))]

    def sum_one(z, base=True):
        for r in chunks:
            pq = [[rows(u, i, s, z, r=r) for s in range(2)] for i in range(3)]
            if base:
                w = sum((DT * S[0][i]) * react(*pq[i]) for i in range(3))
            for s in range(2):
                total = sum((DT * S[0][i]) * pq[i][s] for i in range(3))
                a[s, z, 8 + r : 8 + r + ROWS, :] = total
                if base:
                    s1[s, z, r : r + ROWS, :] = pq[0][s] + SIGN[s] * w - DECAY[s] * total

    def sum_two(z, base=True):
        weight = (DT * S[1][0], DT * S[1][1] - H, DT * S[1][2])
        for r in chunks:
            pq = [[rows(u, i, s, z, r=r) for s in range(2)] for i in range(3)]
            ab = [rows(s1, s, z, r=r) for s in range(2)]
            if base:
                w = H * react(*ab) + sum(weight[i] * react(*pq[i]) for i in range(3))
            for s in range(2):
                total = H * ab[s] + sum(weight[i] * pq[i][s] for i in range(3))
                a[s, z, 8 + r : 8 + r + ROWS, :] = total
                if base:
                    s2[s, z - 1, r : r + ROWS, :] = ab[s] + SIGN[s] * w - DECAY[s] * total

    def diffuse(ref, z, shift):
        for r in chunks:
            for s in range(2):
                around, mid = sides(s, z, r)
                below = a[s, z - 1, 8 + r : 8 + r + ROWS, :]
                above = a[s, z + 1, 8 + r : 8 + r + ROWS, :]
                lap = around + (below + above) - 6.0 * mid
                ref[s, z - shift, r : r + ROWS, :] = (
                    ref[s, z - shift, r : r + ROWS, :] + DIFFUSE[s] * lap
                )

    loads[0].wait()
    loads[1].wait()
    even = core == 0
    arrived(u.at[0, :, pl.ds(1, 1)], r_u0.at[0])
    arrived(u.at[0, :, pl.ds(4, 1)], r_u0.at[1])
    send(u.at[0, :, 4], u.at[0, :, 0], r_u0h.at[0], hi, has_hi & even)
    send(u.at[0, :, 1], u.at[0, :, 5], r_u0h.at[1], lo, has_lo & even)
    pl.when(has_lo)(lambda: arrived(u.at[2, :, 0], r_h.at[1, 0]))
    pl.when(has_hi)(lambda: arrived(u.at[2, :, 5], r_h.at[1, 1]))
    send(u.at[2, :, 0], u.at[0, :, 0], r_u0h.at[0], nxt, has_lo & even)
    send(u.at[2, :, 5], u.at[0, :, 5], r_u0h.at[1], nxt, has_hi & even)
    arrived(u.at[0, :, pl.ds(2, 2)], r_u0.at[2])
    for z in (1, 2, 3, 4):
        sum_one(z)
    for z in (2, 3):
        diffuse(s1, z, 0)
    pl.when(has_lo)(lambda: arrived(u.at[1, :, 0], r_h.at[0, 0]))
    pl.when(has_lo)(lambda: arrived(u.at[0, :, 0], r_u0h.at[0]))
    sum_one(0, False)
    diffuse(s1, 1, 0)
    send(s1.at[:, 1], s1.at[:, 5], r_s1.at[1], lo, has_lo)
    pl.when(has_hi)(lambda: arrived(u.at[1, :, 5], r_h.at[0, 1]))
    pl.when(has_hi)(lambda: arrived(u.at[0, :, 5], r_u0h.at[1]))
    sum_one(5, False)
    diffuse(s1, 4, 0)
    send(s1.at[:, 4], s1.at[:, 0], r_s1.at[0], hi, has_hi)

    for z in (1, 2, 3, 4):
        sum_two(z)
    for z in (2, 3):
        diffuse(s2, z, 1)
    pl.when(has_lo)(lambda: arrived(s1.at[:, 0], r_s1.at[0]))
    pl.when(has_hi)(lambda: arrived(s1.at[:, 5], r_s1.at[1]))
    sum_two(0, False)
    sum_two(5, False)
    diffuse(s2, 1, 1)
    diffuse(s2, 4, 1)

    is_first = jnp.where(tm == 0, 1.0, 0.0)
    for i in range(2):
        for j in range(2):
            z = 2 * j + 1
            for r in chunks:
                w = 0.0
                both = [0.0, 0.0]
                keep = [0.0, 0.0]
                for k in (z, z + 1):
                    p0 = [rows(u, 0, s, k, r=r) for s in range(2)]
                    p1 = [rows(s1, s, k, r=r) for s in range(2)]
                    p2 = [rows(s2, s, k - 1, r=r) for s in range(2)]
                    three = (p0, p1, p2)
                    w = w + sum((DT * S[i][t]) * react(*three[t]) for t in range(3))
                    for s in range(2):
                        total = sum((DT * S[i][t]) * three[t][s] for t in range(3))
                        both[s] = both[s] + total
                        if i == 0:
                            keep[s] = keep[s] + is_first * p0[s] - p1[s]
                        else:
                            keep[s] = keep[s] + p1[s] - p2[s]
                for s in range(2):
                    out_of = 0 if j == 0 else 5
                    near = 3 if j == 0 else 2
                    beyond = (DT * S[i][0]) * rows(u, 0, s, out_of, r=r) + (DT * S[i][1]) * rows(
                        s1, s, out_of, r=r
                    )
                    beyond = beyond + (
                        (DT * S[i][0]) * rows(u, 0, s, near, r=r)
                        + (DT * S[i][1]) * rows(s1, s, near, r=r)
                        + (DT * S[i][2]) * rows(s2, s, near - 1, r=r)
                    )
                    a[s, j, 8 + r : 8 + r + ROWS, :] = both[s]
                    g[i, j, r : r + ROWS, s * n : (s + 1) * n] = (
                        keep[s]
                        + SIGN[s] * w
                        - DECAY[s] * both[s]
                        + DIFFUSE[s] * (beyond - 5.0 * both[s])
                    )
            for r in chunks:
                for s in range(2):
                    around, _ = sides(s, j, r)
                    at_s = slice(s * n, (s + 1) * n)
                    g[i, j, r : r + ROWS, at_s] = (
                        g[i, j, r : r + ROWS, at_s] + DIFFUSE[s] * around
                    )
    for j in range(2):
        for r in chunks:
            for s in range(2):
                at_s = slice(s * n, (s + 1) * n)
                g[2, j, r : r + ROWS, at_s] = DIFFUSE[s] * rows(s2, s, 3 * j, r=r)
                g[3, j, r : r + ROWS, at_s] = rows(s2, s, 2 * j, r=r) + rows(s2, s, 2 * j + 1, r=r)

    for load in loads[2:]:
        load.wait()

    def to_modes(i):
        both = jnp.concatenate([g[i, 0], g[i, 1]], axis=0)
        along_x = left(fx, both)
        for s in range(2):
            at_s = slice(s * n, (s + 1) * n)
            wide = jnp.concatenate([along_x[: n // 2, at_s], along_x[n // 2 :, at_s]], axis=1)
            modes = right(wide, fy)
            if i == 3:
                c2out[s] = modes
            else:
                spec[s, :, (i + 2) % 3] = modes.reshape(spaces, part, n)

    part = n // 2 // spaces
    to_modes(3)
    send(c2out, c2in, r_c2, nxt, has_next)
    to_modes(1)
    to_modes(2)
    waits_for(0, above_far)

    def exchange(k, fields):
        for d in yc:
            y, c = owner(d)
            send(
                spec.at[c, y, fields], gather.at[core, sp, fields], r_in.at[k, core, sp],
                (chip * 2 + c, y),
            )

    exchange(0, pl.ds(0, 2))
    to_modes(0)
    pl.when(has_prior)(lambda: arrived(c2in, r_c2))
    for s in range(2):
        spec[s, :, 2] = spec[s, :, 2] + c2in[s].reshape(spaces, part, n)
    exchange(1, pl.ds(2, 1))
    gather[core, sp] = spec[core, sp]
    for k, fields in ((0, pl.ds(0, 2)), (1, pl.ds(2, 1))):
        for d in yc:
            y, c = owner(d)
            arrived(gather.at[c, y, fields], r_in.at[k, c, y])

    m = n // 2
    power = pw[...]
    square = power * power
    d0, d1 = [], []
    for c in range(2):
        own = [gather[c, :, i].reshape(m, n) for i in range(3)]
        d0.append(left(m0, jnp.concatenate([own[2], own[1]], axis=0)))
        d1.append(left(m1, jnp.concatenate([own[0], own[1]], axis=0)))
    e = [power * (power * d0[c] + d1[c]) for c in range(2)]
    e2[...] = square * e[0] + e[1]

    share = m // chips_x

    def shared(x):
        return pl.ds(pl.multiple_of(x * share, share), share)

    waits_for(1, chips_x - 1 - cx)
    for x in x_peers:
        send(e2.at[shared(x)], xin.at[cx], r_x.at[cx], (at(cz, x, core), sp))
    xin[cx] = e2[shared(cx)]
    for x in x_peers:
        arrived(xin.at[x], r_x.at[x])
    p1 = pw[shared(cx)]
    p2 = p1 * p1
    p4 = p2 * p2
    running = jnp.zeros((share, n), jnp.float32)
    before, ahead = [], []
    power_x = jnp.ones((share, n), jnp.float32)
    for x in range(chips_x):
        before.append(running)
        ahead.append(power_x)
        running = p4 * running + xin[x]
        power_x = power_x * p4
    tot[...] = running
    waits_for(2, chips_z - 1 - cz)
    for z in reversed(range(1, chips_z)):
        send(tot, zin.at[cz], r_z.at[cz], (at(z, cx, core), sp), z > cz)

    def add_group(z, earlier):
        arrived(zin.at[z], r_z.at[z])
        return power_x * earlier + zin[z]

    earlier = lax.fori_loop(0, cz, add_group, jnp.zeros((share, n), jnp.float32))
    for x in range(chips_x):
        back[x] = ahead[x] * earlier + before[x]
    for x in x_peers:
        send(back.at[x], pre.at[shared(cx)], r_b.at[cx], (at(cz, x, core), sp))
    pre[shared(cx)] = back[cx]
    for x in x_peers:
        arrived(pre.at[shared(x)], r_b.at[x])

    change = pre[...]
    for c in range(2):
        for f, source in enumerate((d0[c], d1[c])):
            change = power * (change + source)
            fine[c, :, f] = left(nz, change).reshape(spaces, 2 * part, n)

    for d in yc:
        y, c = owner(d)
        send(fine.at[c, y], fin.at[core, sp], r_f.at[core, sp], (chip * 2 + c, y))
    fin[core, sp] = fine[core, sp]
    for d in yc:
        y, c = owner(d)
        arrived(fin.at[c, y], r_f.at[c, y])

    for f in range(2):
        tall = []
        for s in range(2):
            wide = right(fin[s, :, f].reshape(n, n), vy)
            tall.append(jnp.concatenate([wide[:, :n], wide[:, n:]], axis=0))
        refined = left(vx, jnp.concatenate(tall, axis=1))
        for s in range(2):
            for z in range(4):
                piece = refined[z * n : (z + 1) * n, s * n : (s + 1) * n]
                swept = s1[s, z + 1] if f == 0 else s2[s, z]
                out[0, f, s, z] = swept + piece

    for copy, when in sends:
        if when is None:
            copy.wait_send()
        else:
            pl.when(when)(copy.wait_send)


def local(shape, nodes, initial):
    count, spaces, chips_x, chips_z, n = shape
    consts = tables(n, spaces)
    m = n // 2
    part = m // spaces
    share = m // chips_x
    f32 = jnp.float32
    vmem, sem = pltpu.VMEM, pltpu.SemaphoreType.DMA
    n_sends = 4 + 3 + 4 + 2 + 1 + 3 * (2 * spaces - 1) + 2 * (chips_x - 1) + chips_z - 1
    scratch = [
        vmem((3, 2, 6, n, n), f32),
        vmem((2, 6, n, n), f32),
        vmem((2, 4, n, n), f32),
        vmem((2, 6, n + 16, n), f32),
        vmem((4, 2, n, 2 * n), f32),
    ]
    scratch += [vmem(c.shape, jnp.bfloat16) for c in consts[:-1]]
    scratch += [
        vmem((m, n), f32),
        vmem((2, spaces, 3, part, n), f32),
        vmem((2, m, n), f32),
        vmem((2, m, n), f32),
        vmem((2, spaces, 3, part, n), f32),
        vmem((m, n), f32),
        vmem((chips_x, share, n), f32),
        vmem((share, n), f32),
        vmem((chips_z, share, n), f32),
        vmem((chips_x, share, n), f32),
        vmem((m, n), f32),
        vmem((2, spaces, 2, 2 * part, n), f32),
        vmem((2, spaces, 2, 2 * part, n), f32),
        sem((n_sends,)),
        sem((10,)),
        sem((3,)),
        sem((2, 2)),
        sem((2,)),
        sem((2,)),
        sem(()),
        sem((2, 2, spaces)),
        sem((chips_x,)),
        sem((chips_z,)),
        sem((chips_x,)),
        sem((2, spaces)),
        pltpu.SemaphoreType.REGULAR((4,)),
    ]
    operands = [nodes, initial, *[jnp.asarray(c) for c in consts]]
    anywhere = pl.BlockSpec(memory_space=pl.ANY)
    return pl.pallas_call(
        functools.partial(kernel, shape),
        out_shape=jax.ShapeDtypeStruct((1, 2, 2, 4, n, n), f32),
        in_specs=[anywhere] * (2 + len(consts)),
        out_specs=pl.BlockSpec(memory_space=pltpu.VMEM),
        scratch_shapes=scratch,
        compiler_params=pltpu.CompilerParams(
            collective_id=0, has_side_effects=True, vmem_limit_bytes=40 << 20
        ),
        name="iteration",
    )(*[pltpu.with_memory_space_constraint(x, pltpu.HBM) for x in operands])


def solution(mesh):
    count, spaces = mesh.shape["tm"], mesh.shape["space"]
    chips_x = 4 if count == 64 else 2
    chips_z = count // (2 * chips_x)
    in_specs = (P("tm", None, None, "space", None, None), P(None, "space", None, None))
    out_specs = P("tm", None, None, "space", None, None)

    def run(nodes, initial):
        shape = (count, spaces, chips_x, chips_z, nodes.shape[-1])
        return jax.shard_map(
            functools.partial(local, shape),
            mesh=mesh, in_specs=in_specs, out_specs=out_specs, check_vma=False,
        )(nodes, initial)

    return run
```

```python
import functools
import math

import jax
import jax.numpy as jnp
import ml_dtypes
import numpy as np
from jax import lax
from jax.experimental import pallas as pl
from jax.experimental.pallas import tpu as pltpu
from jax.sharding import PartitionSpec as P

MESH = pl.DeviceIdType.MESH
DIFFUSE = (0.5, 0.25)
DECAY = (0.04, 0.1)
SIGN = (-1.0, 1.0)
DT = 0.5
H = 0.25
S = ((5.0 / 24.0, 1.0 / 3.0, -1.0 / 24.0), (-1.0 / 24.0, 1.0 / 3.0, 5.0 / 24.0))
ROWS = 32


def sine_table(points, modes, stretch):
    place = np.arange(points) + 0.5
    order = np.arange(modes) + 1.0
    angle = math.pi / (stretch * modes) * place[:, None] * order[None, :]
    weight = np.where(np.arange(modes) == modes - 1, math.sqrt(0.5), 1.0)
    return math.sqrt(2.0 / modes) * weight[None, :] * np.sin(angle)


def two_parts(table):
    high = table.astype(np.float32).astype(ml_dtypes.bfloat16)
    low = (table - high.astype(np.float64)).astype(np.float32).astype(ml_dtypes.bfloat16)
    return np.stack([high, low])


@functools.lru_cache(maxsize=None)
def tables(n, spaces):
    m, mz = n // 2, 2 * spaces
    half = m // 2
    per = half // spaces
    average = np.kron(np.eye(m), np.array([[0.5, 0.5]]))
    fine = sine_table(m, m, 1.0).T @ average
    fx = np.zeros((2, half, 2, 2, n))
    for z in range(2):
        fx[:, :, z, z, :] = 0.5 * fine.reshape(2, half, n)
    fx = fx.reshape(2 * m, 2 * n)
    fy = np.kron(np.eye(2), fine.T)
    wz = sine_table(mz, mz, 1.0).T
    own = np.zeros((mz, per, spaces, per, 2))
    edge = np.zeros((mz, per, spaces, per, 2))
    for i in range(per):
        for y in range(spaces):
            for z in range(2):
                own[:, i, y, i, z] = wz[:, 2 * y + z]
            if y > 0:
                edge[:, i, y, i, 0] = wz[:, 2 * y - 1]
            if y < spaces - 1:
                edge[:, i, y, i, 1] = wz[:, 2 * y + 2]
    own, edge = own.reshape(m, m), edge.reshape(m, m)
    mats = np.stack(
        [np.concatenate([own, edge * (DT * S[i][2])], axis=1) for i in range(2)]
    )
    nz = np.kron(sine_table(2 * mz, mz, 2.0), np.eye(per))
    vxy = sine_table(n, m, 2.0)
    vy = np.kron(np.eye(2), vxy.T)
    vx = np.zeros((4, n, 2, spaces, 4, per))
    for f in range(4):
        vx[f, :, :, :, f, :] = vxy.reshape(n, 2, spaces, per)
    vx = vx.reshape(4 * n, 2 * spaces * 4 * per)

    def eigen(modes):
        return 2.0 * np.cos(math.pi * (np.arange(modes) + 1.0) / modes) - 2.0

    ab = (eigen(m)[:, None] + eigen(m)[None, :]).reshape(2, spaces, per, m)
    e = (eigen(mz)[None, :, None, None, None] + ab.transpose(1, 2, 0, 3)[:, None]) / 4.0
    lin = np.stack([d * e - k for d, k in zip(DIFFUSE, DECAY)])
    factor = 1.0 / (1.0 - H * lin)
    factor = factor.reshape(2, spaces, m, n).astype(np.float32)
    return tuple(map(two_parts, (fx, fy, mats[0], mats[1], nz, vy, vx))) + (factor,)


def split(x):
    high = x.astype(jnp.bfloat16)
    low = (x - high.astype(jnp.float32)).astype(jnp.bfloat16)
    return high, low


def dot(a, b):
    return jnp.dot(a, b, preferred_element_type=jnp.float32)


def left(table, x):
    high, low = split(x)
    return dot(table[0], high) + (dot(table[0], low) + dot(table[1], high))


def right(x, table):
    high, low = split(x)
    return dot(high, table[0]) + (dot(low, table[0]) + dot(high, table[1]))


def kernel(
    shape,
    nodes, initial, fx_h, fy_h, m0_h, m1_h, nz_h, vy_h, vx_h, p_h,
    out,
    u, s1, s2, a, g, fx, fy, m0, m1, nz, vy, vx, pw,
    sx, rim, spec, c2out, c2in, gather, e2, xin, tot, zin, fine, fin,
    ssem, lsem, r_u0, r_h, r_u0h, r_s1, r_c2, r_in, r_x, r_z, r_f, credit,
):
    count, spaces, chips_x, chips_z, n = shape
    tm, sp = lax.axis_index("tm"), lax.axis_index("space")
    core = lax.rem(tm, 2)
    chip = tm // 2
    cx, cz = lax.rem(chip, chips_x), chip // chips_x
    sends = []

    def at(z, x, c):
        return (z * chips_x + x) * 2 + c

    def send(src, dst, sem, device, when=None):
        copy = pltpu.make_async_remote_copy(
            src, dst, ssem.at[len(sends)], sem, device_id=device, device_id_type=MESH
        )
        sends.append((copy, when))
        if when is None:
            copy.start()
        else:
            pl.when(when)(copy.start)

    def arrived(dst, sem):
        pltpu.make_async_copy(dst, dst, sem).wait()

    has_lo, has_hi = sp > 0, sp < spaces - 1
    lo, hi = (tm, jnp.maximum(sp - 1, 0)), (tm, jnp.minimum(sp + 1, spaces - 1))
    has_next, has_prior = tm < count - 1, tm > 0
    nxt = (lax.rem(tm + 1, count), sp)
    prv = (lax.rem(tm + count - 1, count), sp)
    ring = sorted(range(spaces), key=lambda d: -min(d, spaces - d))
    yc = [(d, c) for d in ring for c in (1, 0) if (d, c) != (0, 0)]

    def owner(d):
        return lax.rem(sp + d[0], spaces), lax.rem(core + d[1], 2)

    x_peers = [lax.rem(cx + d, chips_x) for d in (2, 1, 3) if d < chips_x]
    if chips_x == 2:
        x_peers = [1 - cx]

    loads = [
        pltpu.make_async_copy(nodes.at[0, 0], u.at[1, :, pl.ds(1, 4)], lsem.at[0]),
        pltpu.make_async_copy(nodes.at[0, 1], u.at[2, :, pl.ds(1, 4)], lsem.at[1]),
        pltpu.make_async_copy(fx_h, fx, lsem.at[2]),
        pltpu.make_async_copy(fy_h, fy, lsem.at[3]),
        pltpu.make_async_copy(m0_h, m0, lsem.at[4]),
        pltpu.make_async_copy(m1_h, m1, lsem.at[5]),
        pltpu.make_async_copy(nz_h, nz, lsem.at[6]),
        pltpu.make_async_copy(vy_h, vy, lsem.at[7]),
        pltpu.make_async_copy(vx_h, vx, lsem.at[8]),
        pltpu.make_async_copy(p_h.at[core, sp], pw, lsem.at[9]),
    ]
    for load in loads:
        load.start()
    pieces = [(0, 1), (3, 1), (1, 2)]

    @pl.when(tm == 0)
    def _():
        for i, (z, length) in enumerate(pieces):
            pltpu.make_async_copy(
                initial.at[:, pl.ds(z, length)], u.at[0, :, pl.ds(1 + z, length)], r_u0.at[i]
            ).start()

    barrier = pltpu.get_barrier_semaphore()

    def one(flag):
        return jnp.where(flag, 1, 0)

    sibling = tm + 1 - 2 * core
    crosses = jnp.where(core == 1, cx == chips_x - 1, cx == 0)
    beside = lax.rem(tm + count - 1 + 2 * core, count)
    has_beside = jnp.where(core == 1, has_next, has_prior)

    half = chips_z // 2
    half_at = (cz // half) * half
    ends = cz == half_at + half - 1
    z_first = cz + 1
    z_last = jnp.where(ends, jnp.minimum(half_at + 2 * half, chips_z), half_at + half)
    z_below = cz - half_at + one(half_at > 0)

    def greet(t, y):
        pl.semaphore_signal(barrier, 1, device_id=(t, y), device_id_type=MESH)

    def answer(which, t, y):
        pl.semaphore_signal(credit.at[which], 1, device_id=(t, y), device_id_type=MESH)

    def waits_for(which, answers):
        pl.when(answers > 0)(lambda: pl.semaphore_wait(credit.at[which], answers))

    def over(lower, upper, work):
        def step(i, carry):
            work(i)
            return carry

        lax.fori_loop(lower, upper, step, 0)

    def far_columns(y, call):
        call(sibling, y)
        pl.when((y != sp + 1) & (y != sp - 1))(lambda: call(tm, y))

    pl.when(has_hi)(lambda: greet(tm, hi[1]))
    pl.when(has_lo)(lambda: greet(tm, lo[1]))
    greet(sibling, sp)
    pl.when(has_beside & (~crosses | (core == 1)))(lambda: greet(beside, sp))
    over(sp + 1, spaces, lambda y: far_columns(y, greet))
    over(cx + 1, chips_x, lambda x: greet(at(cz, x, core), sp))
    over(z_first, z_last, lambda z: greet(at(z, cx, core), sp))

    below_far = 2 * sp - one(has_lo)
    above_far = 2 * (spaces - 1 - sp) - one(has_hi)
    pl.semaphore_wait(
        barrier,
        one(has_lo) + one(has_hi) + 1 + one(has_beside & (~crosses | (core == 0)))
        + below_far + cx + z_below,
    )
    pl.when(has_beside & crosses & (core == 0))(lambda: answer(3, beside, sp))

    for node in (2, 1):
        send(nodes.at[0, node - 1, :, 3], u.at[node, :, 0], r_h.at[node - 1, 0], hi, has_hi)
        send(nodes.at[0, node - 1, :, 0], u.at[node, :, 5], r_h.at[node - 1, 1], lo, has_lo)
    waits_for(3, one(has_beside & crosses & (core == 1)))
    for i, (z, length) in enumerate(pieces):
        send(
            nodes.at[0, 1, :, pl.ds(z, length)], u.at[0, :, pl.ds(1 + z, length)],
            r_u0.at[i], nxt, has_next,
        )

    over(0, sp, lambda y: far_columns(y, functools.partial(answer, 0)))
    over(0, cx, lambda x: answer(1, at(cz, x, core), sp))
    over(half_at, cz, lambda z: answer(2, at(z, cx, core), sp))
    pl.when(half_at > 0)(lambda: answer(2, at(half_at - 1, cx, core), sp))

    zero = jnp.zeros((n, n), jnp.float32)
    for s in range(2):
        for z in range(6):
            a[s, z, 0:8, :] = jnp.zeros((8, n), jnp.float32)
            a[s, z, 8 + n : 16 + n, :] = jnp.zeros((8, n), jnp.float32)

    def outside(plane):
        for s in range(2):
            for i in range(3):
                u[i, s, plane] = zero
            s1[s, plane] = zero

    pl.when(sp == 0)(lambda: outside(0))
    pl.when(sp == spaces - 1)(lambda: outside(5))

    @pl.when(tm == 0)
    def _():
        c2in[...] = jnp.zeros(c2in.shape, jnp.float32)

    lane = lax.broadcasted_iota(jnp.int32, (ROWS, n), 1)
    first_lane, last_lane = lane == 0, lane == n - 1
    chunks = range(0, n, ROWS)

    def react(p, q):
        return (1.0 + p) * (q * q)

    def sides(s, z, r):
        mid = a[s, z, 8 + r : 8 + r + ROWS, :]
        west = jnp.where(first_lane, 0.0, pltpu.roll(mid, 1, 1))
        east = jnp.where(last_lane, 0.0, pltpu.roll(mid, n - 1, 1))
        north = a[s, z, 7 + r : 7 + r + ROWS, :]
        south = a[s, z, 9 + r : 9 + r + ROWS, :]
        return (west + east) + (north + south), mid

    def rows(ref, *index, r):
        return ref[(*index, slice(r, r + ROWS), slice(None))]

    def sum_one(z, base=True):
        for r in chunks:
            pq = [[rows(u, i, s, z, r=r) for s in range(2)] for i in range(3)]
            if base:
                w = sum((DT * S[0][i]) * react(*pq[i]) for i in range(3))
            for s in range(2):
                total = sum((DT * S[0][i]) * pq[i][s] for i in range(3))
                a[s, z, 8 + r : 8 + r + ROWS, :] = total
                if base:
                    s1[s, z, r : r + ROWS, :] = pq[0][s] + SIGN[s] * w - DECAY[s] * total

    def sum_two(z, base=True):
        weight = (DT * S[1][0], DT * S[1][1] - H, DT * S[1][2])
        for r in chunks:
            pq = [[rows(u, i, s, z, r=r) for s in range(2)] for i in range(3)]
            ab = [rows(s1, s, z, r=r) for s in range(2)]
            if base:
                w = H * react(*ab) + sum(weight[i] * react(*pq[i]) for i in range(3))
            for s in range(2):
                total = H * ab[s] + sum(weight[i] * pq[i][s] for i in range(3))
                a[s, z, 8 + r : 8 + r + ROWS, :] = total
                if base:
                    s2[s, z - 1, r : r + ROWS, :] = ab[s] + SIGN[s] * w - DECAY[s] * total

    def diffuse(ref, z, shift):
        for r in chunks:
            for s in range(2):
                around, mid = sides(s, z, r)
                below = a[s, z - 1, 8 + r : 8 + r + ROWS, :]
                above = a[s, z + 1, 8 + r : 8 + r + ROWS, :]
                lap = around + (below + above) - 6.0 * mid
                ref[s, z - shift, r : r + ROWS, :] = (
                    ref[s, z - shift, r : r + ROWS, :] + DIFFUSE[s] * lap
                )

    loads[0].wait()
    loads[1].wait()
    even = core == 0
    arrived(u.at[0, :, pl.ds(1, 1)], r_u0.at[0])
    arrived(u.at[0, :, pl.ds(4, 1)], r_u0.at[1])
    send(u.at[0, :, 4], u.at[0, :, 0], r_u0h.at[0], hi, has_hi & even)
    send(u.at[0, :, 1], u.at[0, :, 5], r_u0h.at[1], lo, has_lo & even)
    pl.when(has_lo)(lambda: arrived(u.at[2, :, 0], r_h.at[1, 0]))
    pl.when(has_hi)(lambda: arrived(u.at[2, :, 5], r_h.at[1, 1]))
    send(u.at[2, :, 0], u.at[0, :, 0], r_u0h.at[0], nxt, has_lo & even)
    send(u.at[2, :, 5], u.at[0, :, 5], r_u0h.at[1], nxt, has_hi & even)
    arrived(u.at[0, :, pl.ds(2, 2)], r_u0.at[2])
    for z in (1, 2, 3, 4):
        sum_one(z)
    edges = ((0, 1, 2, 0), (1, 4, 3, 5))
    for k, z, inner, _ in edges:
        for r in chunks:
            for s in range(2):
                around, mid = sides(s, z, r)
                lap = around + a[s, inner, 8 + r : 8 + r + ROWS, :] - 6.0 * mid
                sx[k, s, r : r + ROWS, :] = rows(s1, s, z, r=r) + DIFFUSE[s] * lap
                rim[k, s, r : r + ROWS, :] = DIFFUSE[s] * mid
        if k == 0:
            send(sx.at[0], s1.at[:, 5], r_s1.at[1], lo, has_lo)
        else:
            send(sx.at[1], s1.at[:, 0], r_s1.at[0], hi, has_hi)
    for z in (2, 3):
        diffuse(s1, z, 0)
    for k, z, _, outer in edges:
        has = (has_lo, has_hi)[k]
        ready = [(u.at[1, :, outer], r_h.at[0, k]), (u.at[0, :, outer], r_u0h.at[k])]
        for dst, landed in ready:
            pl.when(has)(functools.partial(arrived, dst, landed))
        sum_one(outer, False)
        for r in chunks:
            for s in range(2):
                beyond = a[s, outer, 8 + r : 8 + r + ROWS, :]
                s1[s, z, r : r + ROWS, :] = sx[k, s, r : r + ROWS, :] + DIFFUSE[s] * beyond

    for z in (1, 2, 3, 4):
        sum_two(z)
    for z in (2, 3):
        diffuse(s2, z, 1)

    def complete(k, outer):
        arrived(s1.at[:, outer], r_s1.at[k])
        for r in chunks:
            for s in range(2):
                s1[s, outer, r : r + ROWS, :] = rows(s1, s, outer, r=r) + rim[k, s, r : r + ROWS, :]

    pl.when(has_lo)(lambda: complete(0, 0))
    sum_two(0, False)
    pl.when(has_hi)(lambda: complete(1, 5))
    sum_two(5, False)
    diffuse(s2, 1, 1)
    diffuse(s2, 4, 1)

    is_first = jnp.where(tm == 0, 1.0, 0.0)
    for i in range(2):
        for j in range(2):
            z = 2 * j + 1
            for r in chunks:
                w = 0.0
                both = [0.0, 0.0]
                keep = [0.0, 0.0]
                for k in (z, z + 1):
                    p0 = [rows(u, 0, s, k, r=r) for s in range(2)]
                    p1 = [rows(s1, s, k, r=r) for s in range(2)]
                    p2 = [rows(s2, s, k - 1, r=r) for s in range(2)]
                    three = (p0, p1, p2)
                    w = w + sum((DT * S[i][t]) * react(*three[t]) for t in range(3))
                    for s in range(2):
                        total = sum((DT * S[i][t]) * three[t][s] for t in range(3))
                        both[s] = both[s] + total
                        if i == 0:
                            keep[s] = keep[s] + is_first * p0[s] - p1[s]
                        else:
                            keep[s] = keep[s] + p1[s] - p2[s]
                for s in range(2):
                    out_of = 0 if j == 0 else 5
                    near = 3 if j == 0 else 2
                    beyond = (DT * S[i][0]) * rows(u, 0, s, out_of, r=r) + (DT * S[i][1]) * rows(
                        s1, s, out_of, r=r
                    )
                    beyond = beyond + (
                        (DT * S[i][0]) * rows(u, 0, s, near, r=r)
                        + (DT * S[i][1]) * rows(s1, s, near, r=r)
                        + (DT * S[i][2]) * rows(s2, s, near - 1, r=r)
                    )
                    a[s, j, 8 + r : 8 + r + ROWS, :] = both[s]
                    g[i, j, r : r + ROWS, s * n : (s + 1) * n] = (
                        keep[s]
                        + SIGN[s] * w
                        - DECAY[s] * both[s]
                        + DIFFUSE[s] * (beyond - 5.0 * both[s])
                    )
            for r in chunks:
                for s in range(2):
                    around, _ = sides(s, j, r)
                    at_s = slice(s * n, (s + 1) * n)
                    g[i, j, r : r + ROWS, at_s] = (
                        g[i, j, r : r + ROWS, at_s] + DIFFUSE[s] * around
                    )
    for j in range(2):
        for r in chunks:
            for s in range(2):
                at_s = slice(s * n, (s + 1) * n)
                g[2, j, r : r + ROWS, at_s] = DIFFUSE[s] * rows(s2, s, 3 * j, r=r)
                g[3, j, r : r + ROWS, at_s] = rows(s2, s, 2 * j, r=r) + rows(s2, s, 2 * j + 1, r=r)

    for load in loads[2:]:
        load.wait()

    def to_modes(i):
        both = jnp.concatenate([g[i, 0], g[i, 1]], axis=0)
        along_x = left(fx, both)
        for s in range(2):
            at_s = slice(s * n, (s + 1) * n)
            wide = jnp.concatenate([along_x[: n // 2, at_s], along_x[n // 2 :, at_s]], axis=1)
            modes = right(wide, fy)
            if i == 3:
                c2out[s] = modes
            else:
                spec[s, :, (i + 2) % 3] = modes.reshape(spaces, part, n)

    part = n // 2 // spaces
    to_modes(3)
    send(c2out, c2in, r_c2, nxt, has_next)
    to_modes(1)
    to_modes(2)
    waits_for(0, above_far)

    def exchange(k, fields):
        for d in yc:
            y, c = owner(d)
            send(
                spec.at[c, y, fields], gather.at[core, sp, fields], r_in.at[k, core, sp],
                (chip * 2 + c, y),
            )

    exchange(0, pl.ds(0, 2))
    to_modes(0)
    pl.when(has_prior)(lambda: arrived(c2in, r_c2))
    for s in range(2):
        spec[s, :, 2] = spec[s, :, 2] + c2in[s].reshape(spaces, part, n)
    exchange(1, pl.ds(2, 1))
    gather[core, sp] = spec[core, sp]
    for k, fields in ((0, pl.ds(0, 2)), (1, pl.ds(2, 1))):
        for d in yc:
            y, c = owner(d)
            arrived(gather.at[c, y, fields], r_in.at[k, c, y])

    m = n // 2
    power = pw[...]
    square = power * power
    d0, d1 = [], []
    for c in range(2):
        own = [gather[c, :, i].reshape(m, n) for i in range(3)]
        d0.append(left(m0, jnp.concatenate([own[2], own[1]], axis=0)))
        d1.append(left(m1, jnp.concatenate([own[0], own[1]], axis=0)))
    e = [power * (power * d0[c] + d1[c]) for c in range(2)]
    e2[...] = square * e[0] + e[1]

    waits_for(1, chips_x - 1 - cx)
    for x in x_peers:
        send(e2, xin.at[cx], r_x.at[cx], (at(cz, x, core), sp))
    xin[cx] = e2[...]
    p4 = square * square
    p16 = p4
    for _ in range(chips_x - 1):
        p16 = p16 * p4
    for x in x_peers:
        arrived(xin.at[x], r_x.at[x])

    def add_chip(x, carry):
        running, ahead = carry
        return p4 * running + xin[x], p4 * ahead

    start = (jnp.zeros((m, n), jnp.float32), jnp.ones((m, n), jnp.float32))
    before, ahead = lax.fori_loop(0, cx, add_chip, start)
    total, _ = lax.fori_loop(cx, chips_x, add_chip, (before, ahead))
    waits_for(2, z_last - z_first)

    later = [(cz + d, at(jnp.minimum(cz + d, chips_z - 1), cx, core)) for d in range(1, half + 1)]

    @pl.when(~ends)
    def _():
        tot[...] = total

    for z, t in later[:-1]:
        send(tot, zin.at[cz - half_at], r_z.at[cz - half_at], (t, sp), ~ends & (z < z_last))

    @pl.when(half_at == 0)
    def _():
        zin[half] = jnp.zeros((m, n), jnp.float32)

    pl.when(half_at > 0)(lambda: arrived(zin.at[half], r_z.at[half]))

    def add_group(z, earlier):
        arrived(zin.at[z], r_z.at[z])
        return p16 * earlier + zin[z]

    earlier = lax.fori_loop(0, cz - half_at, add_group, zin[half])

    @pl.when(ends)
    def _():
        tot[...] = p16 * earlier + total

    for z, t in later:
        send(tot, zin.at[half], r_z.at[half], (t, sp), ends & (z < z_last))

    change = ahead * earlier + before
    for c in range(2):
        for f, source in enumerate((d0[c], d1[c])):
            change = power * (change + source)
            fine[c, :, f] = left(nz, change).reshape(spaces, 2 * part, n)

    for d in yc:
        y, c = owner(d)
        send(fine.at[c, y], fin.at[core, sp], r_f.at[core, sp], (chip * 2 + c, y))
    fin[core, sp] = fine[core, sp]
    for d in yc:
        y, c = owner(d)
        arrived(fin.at[c, y], r_f.at[c, y])

    for f in range(2):
        tall = []
        for s in range(2):
            wide = right(fin[s, :, f].reshape(n, n), vy)
            tall.append(jnp.concatenate([wide[:, :n], wide[:, n:]], axis=0))
        refined = left(vx, jnp.concatenate(tall, axis=1))
        for s in range(2):
            for z in range(4):
                piece = refined[z * n : (z + 1) * n, s * n : (s + 1) * n]
                swept = s1[s, z + 1] if f == 0 else s2[s, z]
                out[0, f, s, z] = swept + piece

    for copy, when in sends:
        if when is None:
            copy.wait_send()
        else:
            pl.when(when)(copy.wait_send)


def local(shape, nodes, initial):
    count, spaces, chips_x, chips_z, n = shape
    consts = tables(n, spaces)
    m = n // 2
    part = m // spaces
    f32 = jnp.float32
    vmem, sem = pltpu.VMEM, pltpu.SemaphoreType.DMA
    n_sends = 4 + 3 + 4 + 2 + 1 + 3 * (2 * spaces - 1) + chips_x - 1 + chips_z - 1
    scratch = [
        vmem((3, 2, 6, n, n), f32),
        vmem((2, 6, n, n), f32),
        vmem((2, 4, n, n), f32),
        vmem((2, 6, n + 16, n), f32),
        vmem((4, 2, n, 2 * n), f32),
    ]
    scratch += [vmem(c.shape, jnp.bfloat16) for c in consts[:-1]]
    scratch += [
        vmem((m, n), f32),
        vmem((2, 2, n, n), f32),
        vmem((2, 2, n, n), f32),
        vmem((2, spaces, 3, part, n), f32),
        vmem((2, m, n), f32),
        vmem((2, m, n), f32),
        vmem((2, spaces, 3, part, n), f32),
        vmem((m, n), f32),
        vmem((chips_x, m, n), f32),
        vmem((m, n), f32),
        vmem((chips_z // 2 + 1, m, n), f32),
        vmem((2, spaces, 2, 2 * part, n), f32),
        vmem((2, spaces, 2, 2 * part, n), f32),
        sem((n_sends,)),
        sem((10,)),
        sem((3,)),
        sem((2, 2)),
        sem((2,)),
        sem((2,)),
        sem(()),
        sem((2, 2, spaces)),
        sem((chips_x,)),
        sem((chips_z // 2 + 1,)),
        sem((2, spaces)),
        pltpu.SemaphoreType.REGULAR((4,)),
    ]
    operands = [nodes, initial, *[jnp.asarray(c) for c in consts]]
    anywhere = pl.BlockSpec(memory_space=pl.ANY)
    return pl.pallas_call(
        functools.partial(kernel, shape),
        out_shape=jax.ShapeDtypeStruct((1, 2, 2, 4, n, n), f32),
        in_specs=[anywhere] * (2 + len(consts)),
        out_specs=pl.BlockSpec(memory_space=pltpu.VMEM),
        scratch_shapes=scratch,
        compiler_params=pltpu.CompilerParams(
            collective_id=0, has_side_effects=True, vmem_limit_bytes=40 << 20
        ),
        name="iteration",
    )(*[pltpu.with_memory_space_constraint(x, pltpu.HBM) for x in operands])


def solution(mesh):
    count, spaces = mesh.shape["tm"], mesh.shape["space"]
    chips_x = 4 if count == 64 else 2
    chips_z = count // (2 * chips_x)
    in_specs = (P("tm", None, None, "space", None, None), P(None, "space", None, None))
    out_specs = P("tm", None, None, "space", None, None)

    def run(nodes, initial):
        shape = (count, spaces, chips_x, chips_z, nodes.shape[-1])
        return jax.shard_map(
            functools.partial(local, shape),
            mesh=mesh, in_specs=in_specs, out_specs=out_specs, check_vma=False,
        )(nodes, initial)

    return run
```

```python
import functools
import math

import jax
import jax.numpy as jnp
import ml_dtypes
import numpy as np
from jax import lax
from jax.experimental import pallas as pl
from jax.experimental.pallas import tpu as pltpu
from jax.sharding import PartitionSpec as P

MESH = pl.DeviceIdType.MESH
DIFFUSE = (0.5, 0.25)
DECAY = (0.04, 0.1)
SIGN = (-1.0, 1.0)
DT = 0.5
H = 0.25
S = ((5.0 / 24.0, 1.0 / 3.0, -1.0 / 24.0), (-1.0 / 24.0, 1.0 / 3.0, 5.0 / 24.0))
ROWS = 32


def sine_table(points, modes, stretch):
    place = np.arange(points) + 0.5
    order = np.arange(modes) + 1.0
    angle = math.pi / (stretch * modes) * place[:, None] * order[None, :]
    weight = np.where(np.arange(modes) == modes - 1, math.sqrt(0.5), 1.0)
    return math.sqrt(2.0 / modes) * weight[None, :] * np.sin(angle)


def two_parts(table):
    high = table.astype(np.float32).astype(ml_dtypes.bfloat16)
    low = (table - high.astype(np.float64)).astype(np.float32).astype(ml_dtypes.bfloat16)
    return np.stack([high, low])


@functools.lru_cache(maxsize=None)
def tables(n, spaces):
    m, mz = n // 2, 2 * spaces
    half = m // 2
    per = half // spaces
    average = np.kron(np.eye(m), np.array([[0.5, 0.5]]))
    fine = sine_table(m, m, 1.0).T @ average
    fx = np.zeros((2, half, 2, 2, n))
    for z in range(2):
        fx[:, :, z, z, :] = 0.5 * fine.reshape(2, half, n)
    fx = fx.reshape(2 * m, 2 * n)
    fy = np.kron(np.eye(2), fine.T)
    wz = sine_table(mz, mz, 1.0).T
    own = np.zeros((mz, per, spaces, per, 2))
    edge = np.zeros((mz, per, spaces, per, 2))
    for i in range(per):
        for y in range(spaces):
            for z in range(2):
                own[:, i, y, i, z] = wz[:, 2 * y + z]
            if y > 0:
                edge[:, i, y, i, 0] = wz[:, 2 * y - 1]
            if y < spaces - 1:
                edge[:, i, y, i, 1] = wz[:, 2 * y + 2]
    own, edge = own.reshape(m, m), edge.reshape(m, m)
    mats = np.concatenate([own, edge], axis=1)
    nz = np.kron(sine_table(2 * mz, mz, 2.0), np.eye(per))
    vxy = sine_table(n, m, 2.0)
    vy = np.kron(np.eye(2), vxy.T)
    vx = np.zeros((4, n, 2, spaces, 4, per))
    for f in range(4):
        vx[f, :, :, :, f, :] = vxy.reshape(n, 2, spaces, per)
    vx = vx.reshape(4 * n, 2 * spaces * 4 * per)

    def eigen(modes):
        return 2.0 * np.cos(math.pi * (np.arange(modes) + 1.0) / modes) - 2.0

    ab = (eigen(m)[:, None] + eigen(m)[None, :]).reshape(2, spaces, per, m)
    e = (eigen(mz)[None, :, None, None, None] + ab.transpose(1, 2, 0, 3)[:, None]) / 4.0
    lin = np.stack([d * e - k for d, k in zip(DIFFUSE, DECAY)])
    factor = 1.0 / (1.0 - H * lin)
    factor = factor.reshape(2, spaces, m, n).astype(np.float32)
    return tuple(map(two_parts, (fx, fy, mats, nz, vy, vx))) + (factor,)


def split(x):
    high = x.astype(jnp.bfloat16)
    low = (x - high.astype(jnp.float32)).astype(jnp.bfloat16)
    return high, low


def dot(a, b):
    return jnp.dot(a, b, preferred_element_type=jnp.float32)


def left(table, x):
    high, low = split(x)
    return dot(table[0], high) + (dot(table[0], low) + dot(table[1], high))


def right(x, table):
    high, low = split(x)
    return dot(high, table[0]) + (dot(low, table[0]) + dot(high, table[1]))


def kernel(
    shape,
    nodes, initial, fx_h, fy_h, mz_h, nz_h, vy_h, vx_h, p_h,
    out,
    u, s1, s2, a, g, fx, fy, mz, nz, vy, vx, pw,
    sx, rim, spec, c2out, c2in, gather, e2, xin, tot, zin, fine, fin,
    ssem, lsem, r_u0, r_h, r_u0h, r_s1, r_c2, r_in, r_x, r_z, r_f, credit,
):
    count, spaces, chips_x, chips_z, n = shape
    tm, sp = lax.axis_index("tm"), lax.axis_index("space")
    core = lax.rem(tm, 2)
    chip = tm // 2
    cx, cz = lax.rem(chip, chips_x), chip // chips_x
    sends = []

    def at(z, x, c):
        return (z * chips_x + x) * 2 + c

    def send(src, dst, sem, device, when=None):
        copy = pltpu.make_async_remote_copy(
            src, dst, ssem.at[len(sends)], sem, device_id=device, device_id_type=MESH
        )
        sends.append((copy, when))
        if when is None:
            copy.start()
        else:
            pl.when(when)(copy.start)

    def finish(first, last=None):
        for copy, when in sends[first:last]:
            if when is None:
                copy.wait_send()
            else:
                pl.when(when)(copy.wait_send)

    def arrived(dst, sem):
        pltpu.make_async_copy(dst, dst, sem).wait()

    has_lo, has_hi = sp > 0, sp < spaces - 1
    lo, hi = (tm, jnp.maximum(sp - 1, 0)), (tm, jnp.minimum(sp + 1, spaces - 1))
    has_next, has_prior = tm < count - 1, tm > 0
    nxt = (lax.rem(tm + 1, count), sp)
    prv = (lax.rem(tm + count - 1, count), sp)
    ring = sorted(range(spaces), key=lambda d: -min(d, spaces - d))
    yc = [(d, c) for d in ring for c in (1, 0) if (d, c) != (0, 0)]

    def owner(d):
        return lax.rem(sp + d[0], spaces), lax.rem(core + d[1], 2)

    x_peers = [lax.rem(cx + d, chips_x) for d in (2, 1, 3) if d < chips_x]
    if chips_x == 2:
        x_peers = [1 - cx]

    loads = [
        pltpu.make_async_copy(nodes.at[0, 0], u.at[1, :, pl.ds(1, 4)], lsem.at[0]),
        pltpu.make_async_copy(nodes.at[0, 1], u.at[2, :, pl.ds(1, 4)], lsem.at[1]),
        pltpu.make_async_copy(fx_h, fx, lsem.at[2]),
        pltpu.make_async_copy(fy_h, fy, lsem.at[3]),
        pltpu.make_async_copy(mz_h, mz, lsem.at[4]),
        pltpu.make_async_copy(nz_h, nz, lsem.at[5]),
        pltpu.make_async_copy(vy_h, vy, lsem.at[6]),
        pltpu.make_async_copy(vx_h, vx, lsem.at[7]),
        pltpu.make_async_copy(p_h.at[core, sp], pw, lsem.at[8]),
    ]
    for load in loads:
        load.start()
    pieces = [(0, 1), (3, 1), (1, 2)]

    @pl.when(tm == 0)
    def _():
        for i, (z, length) in enumerate(pieces):
            pltpu.make_async_copy(
                initial.at[:, pl.ds(z, length)], u.at[0, :, pl.ds(1 + z, length)], r_u0.at[i]
            ).start()

    barrier = pltpu.get_barrier_semaphore()

    def one(flag):
        return jnp.where(flag, 1, 0)

    sibling = tm + 1 - 2 * core
    beside = lax.rem(tm + count - 1 + 2 * core, count)
    has_beside = jnp.where(core == 1, has_next, has_prior)

    half = chips_z // 2
    half_at = (cz // half) * half
    ends = cz == half_at + half - 1
    z_first = cz + 1
    z_last = jnp.where(ends, jnp.minimum(half_at + 2 * half, chips_z), half_at + half)
    z_below = cz - half_at + one(half_at > 0)

    def greet(t, y):
        pl.semaphore_signal(barrier, 1, device_id=(t, y), device_id_type=MESH)

    def answer(which, t, y):
        pl.semaphore_signal(credit.at[which], 1, device_id=(t, y), device_id_type=MESH)

    def waits_for(which, answers):
        pl.when(answers > 0)(lambda: pl.semaphore_wait(credit.at[which], answers))

    def over(lower, upper, work):
        def step(i, carry):
            work(i)
            return carry

        lax.fori_loop(lower, upper, step, 0)

    def far_columns(y, call):
        call(sibling, y)
        pl.when((y != sp + 1) & (y != sp - 1))(lambda: call(tm, y))

    pl.when(has_hi)(lambda: greet(tm, hi[1]))
    pl.when(has_lo)(lambda: greet(tm, lo[1]))
    greet(sibling, sp)
    pl.when(has_beside)(lambda: greet(beside, sp))
    over(sp + 1, spaces, lambda y: far_columns(y, greet))
    over(cx + 1, chips_x, lambda x: greet(at(cz, x, core), sp))
    over(z_first, z_last, lambda z: greet(at(z, cx, core), sp))

    below_far = 2 * sp - one(has_lo)
    above_far = 2 * (spaces - 1 - sp) - one(has_hi)
    pl.semaphore_wait(
        barrier,
        one(has_lo) + one(has_hi) + 1 + one(has_beside)
        + below_far + cx + z_below,
    )

    for node in (2, 1):
        send(nodes.at[0, node - 1, :, 3], u.at[node, :, 0], r_h.at[node - 1, 0], hi, has_hi)
        send(nodes.at[0, node - 1, :, 0], u.at[node, :, 5], r_h.at[node - 1, 1], lo, has_lo)
    for i, (z, length) in enumerate(pieces):
        send(
            nodes.at[0, 1, :, pl.ds(z, length)], u.at[0, :, pl.ds(1 + z, length)],
            r_u0.at[i], nxt, has_next,
        )

    over(0, sp, lambda y: far_columns(y, functools.partial(answer, 0)))
    over(0, cx, lambda x: answer(1, at(cz, x, core), sp))
    over(half_at, cz, lambda z: answer(2, at(z, cx, core), sp))
    pl.when(half_at > 0)(lambda: answer(2, at(half_at - 1, cx, core), sp))

    zero = jnp.zeros((n, n), jnp.float32)
    for s in range(2):
        for z in range(6):
            a[s, z, 0:8, :] = jnp.zeros((8, n), jnp.float32)
            a[s, z, 8 + n : 16 + n, :] = jnp.zeros((8, n), jnp.float32)

    def outside(plane):
        for s in range(2):
            for i in range(3):
                u[i, s, plane] = zero
            s1[s, plane] = zero

    pl.when(sp == 0)(lambda: outside(0))
    pl.when(sp == spaces - 1)(lambda: outside(5))

    @pl.when(tm == 0)
    def _():
        c2in[...] = jnp.zeros(c2in.shape, jnp.float32)

    lane = lax.broadcasted_iota(jnp.int32, (ROWS, n), 1)
    first_lane, last_lane = lane == 0, lane == n - 1
    chunks = range(0, n, ROWS)

    def react(p, q):
        return (1.0 + p) * (q * q)

    def sides(s, z, r):
        mid = a[s, z, 8 + r : 8 + r + ROWS, :]
        west = jnp.where(first_lane, 0.0, pltpu.roll(mid, 1, 1))
        east = jnp.where(last_lane, 0.0, pltpu.roll(mid, n - 1, 1))
        north = a[s, z, 7 + r : 7 + r + ROWS, :]
        south = a[s, z, 9 + r : 9 + r + ROWS, :]
        return (west + east) + (north + south), mid

    def rows(ref, *index, r):
        return ref[(*index, slice(r, r + ROWS), slice(None))]

    def sum_one(z, base=True):
        for r in chunks:
            pq = [[rows(u, i, s, z, r=r) for s in range(2)] for i in range(3)]
            if base:
                w = sum((DT * S[0][i]) * react(*pq[i]) for i in range(3))
            for s in range(2):
                total = sum((DT * S[0][i]) * pq[i][s] for i in range(3))
                a[s, z, 8 + r : 8 + r + ROWS, :] = total
                if base:
                    s1[s, z, r : r + ROWS, :] = pq[0][s] + SIGN[s] * w - DECAY[s] * total

    def sum_two(z, base=True):
        weight = (DT * S[1][0], DT * S[1][1] - H, DT * S[1][2])
        for r in chunks:
            pq = [[rows(u, i, s, z, r=r) for s in range(2)] for i in range(3)]
            ab = [rows(s1, s, z, r=r) for s in range(2)]
            if base:
                w = H * react(*ab) + sum(weight[i] * react(*pq[i]) for i in range(3))
            for s in range(2):
                total = H * ab[s] + sum(weight[i] * pq[i][s] for i in range(3))
                a[s, z, 8 + r : 8 + r + ROWS, :] = total
                if base:
                    s2[s, z - 1, r : r + ROWS, :] = ab[s] + SIGN[s] * w - DECAY[s] * total

    def diffuse(ref, z, shift):
        for r in chunks:
            for s in range(2):
                around, mid = sides(s, z, r)
                below = a[s, z - 1, 8 + r : 8 + r + ROWS, :]
                above = a[s, z + 1, 8 + r : 8 + r + ROWS, :]
                lap = around + (below + above) - 6.0 * mid
                ref[s, z - shift, r : r + ROWS, :] = (
                    ref[s, z - shift, r : r + ROWS, :] + DIFFUSE[s] * lap
                )

    loads[0].wait()
    loads[1].wait()
    arrived(u.at[0, :, pl.ds(1, 1)], r_u0.at[0])
    arrived(u.at[0, :, pl.ds(4, 1)], r_u0.at[1])
    send(u.at[0, :, 4], u.at[0, :, 0], r_u0h.at[0], hi, has_hi & ~has_prior)
    send(u.at[0, :, 1], u.at[0, :, 5], r_u0h.at[1], lo, has_lo & ~has_prior)
    pl.when(has_lo)(lambda: arrived(u.at[2, :, 0], r_h.at[1, 0]))
    pl.when(has_hi)(lambda: arrived(u.at[2, :, 5], r_h.at[1, 1]))
    send(u.at[2, :, 0], u.at[0, :, 0], r_u0h.at[0], nxt, has_lo & has_next)
    send(u.at[2, :, 5], u.at[0, :, 5], r_u0h.at[1], nxt, has_hi & has_next)
    arrived(u.at[0, :, pl.ds(2, 2)], r_u0.at[2])
    for z in (1, 2, 3, 4):
        sum_one(z)
    edges = ((0, 1, 2, 0), (1, 4, 3, 5))
    for k, z, inner, _ in edges:
        for r in chunks:
            for s in range(2):
                around, mid = sides(s, z, r)
                lap = around + a[s, inner, 8 + r : 8 + r + ROWS, :] - 6.0 * mid
                sx[k, s, r : r + ROWS, :] = rows(s1, s, z, r=r) + DIFFUSE[s] * lap
                rim[k, s, r : r + ROWS, :] = DIFFUSE[s] * mid
        if k == 0:
            send(sx.at[0], s1.at[:, 5], r_s1.at[1], lo, has_lo)
        else:
            send(sx.at[1], s1.at[:, 0], r_s1.at[0], hi, has_hi)
    for z in (2, 3):
        diffuse(s1, z, 0)
    for k, z, _, outer in edges:
        has = (has_lo, has_hi)[k]
        ready = [(u.at[1, :, outer], r_h.at[0, k]), (u.at[0, :, outer], r_u0h.at[k])]
        for dst, landed in ready:
            pl.when(has)(functools.partial(arrived, dst, landed))
        sum_one(outer, False)
        for r in chunks:
            for s in range(2):
                beyond = a[s, outer, 8 + r : 8 + r + ROWS, :]
                s1[s, z, r : r + ROWS, :] = sx[k, s, r : r + ROWS, :] + DIFFUSE[s] * beyond

    for z in (1, 2, 3, 4):
        sum_two(z)
    for z in (2, 3):
        diffuse(s2, z, 1)

    def complete(k, outer):
        arrived(s1.at[:, outer], r_s1.at[k])
        for r in chunks:
            for s in range(2):
                s1[s, outer, r : r + ROWS, :] = rows(s1, s, outer, r=r) + rim[k, s, r : r + ROWS, :]

    pl.when(has_lo)(lambda: complete(0, 0))
    sum_two(0, False)
    pl.when(has_hi)(lambda: complete(1, 5))
    sum_two(5, False)
    diffuse(s2, 1, 1)
    diffuse(s2, 4, 1)

    is_first = jnp.where(tm == 0, 1.0, 0.0)
    for i in range(2):
        for j in range(2):
            z = 2 * j + 1
            for r in chunks:
                w = 0.0
                both = [0.0, 0.0]
                keep = [0.0, 0.0]
                for k in (z, z + 1):
                    p0 = [rows(u, 0, s, k, r=r) for s in range(2)]
                    p1 = [rows(s1, s, k, r=r) for s in range(2)]
                    p2 = [rows(s2, s, k - 1, r=r) for s in range(2)]
                    three = (p0, p1, p2)
                    w = w + sum((DT * S[i][t]) * react(*three[t]) for t in range(3))
                    for s in range(2):
                        total = sum((DT * S[i][t]) * three[t][s] for t in range(3))
                        both[s] = both[s] + total
                        if i == 0:
                            keep[s] = keep[s] + is_first * p0[s] - p1[s]
                        else:
                            keep[s] = keep[s] + p1[s] - p2[s]
                for s in range(2):
                    out_of = 0 if j == 0 else 5
                    near = 3 if j == 0 else 2
                    beyond = (DT * S[i][0]) * rows(u, 0, s, out_of, r=r) + (DT * S[i][1]) * rows(
                        s1, s, out_of, r=r
                    )
                    beyond = beyond + (
                        (DT * S[i][0]) * rows(u, 0, s, near, r=r)
                        + (DT * S[i][1]) * rows(s1, s, near, r=r)
                        + (DT * S[i][2]) * rows(s2, s, near - 1, r=r)
                    )
                    a[s, j, 8 + r : 8 + r + ROWS, :] = both[s]
                    g[i, j, r : r + ROWS, s * n : (s + 1) * n] = (
                        keep[s]
                        + SIGN[s] * w
                        - DECAY[s] * both[s]
                        + DIFFUSE[s] * (beyond - 5.0 * both[s])
                    )
            for r in chunks:
                for s in range(2):
                    around, _ = sides(s, j, r)
                    at_s = slice(s * n, (s + 1) * n)
                    g[i, j, r : r + ROWS, at_s] = (
                        g[i, j, r : r + ROWS, at_s] + DIFFUSE[s] * around
                    )
    for j in range(2):
        for r in chunks:
            for s in range(2):
                at_s = slice(s * n, (s + 1) * n)
                g[2, j, r : r + ROWS, at_s] = DIFFUSE[s] * rows(s2, s, 3 * j, r=r)
                g[3, j, r : r + ROWS, at_s] = rows(s2, s, 2 * j, r=r) + rows(s2, s, 2 * j + 1, r=r)

    for load in loads[2:]:
        load.wait()

    def to_modes(fields):
        both = [jnp.concatenate([g[i, 0], g[i, 1]], axis=0) for i in fields]
        along_x = left(fx, jnp.concatenate(both, axis=1))
        half_rows = n // 2
        wide = jnp.concatenate(
            [
                jnp.concatenate(
                    [along_x[:half_rows, k * n : (k + 1) * n], along_x[half_rows:, k * n : (k + 1) * n]],
                    axis=1,
                )
                for k in range(2 * len(fields))
            ],
            axis=0,
        )
        modes = right(wide, fy)
        return [modes[k * half_rows : (k + 1) * half_rows] for k in range(2 * len(fields))]

    part = n // 2 // spaces
    ends_modes = to_modes([3])
    for s in range(2):
        c2out[s] = ends_modes[s]
    send(c2out, c2in, r_c2, nxt, has_next)
    others = to_modes([1, 2, 0])
    for i in range(3):
        for s in range(2):
            spec[s, :, i] = others[2 * i + s].reshape(spaces, part, n)
    waits_for(0, above_far)

    def exchange(k, fields):
        for d in yc:
            y, c = owner(d)
            send(
                spec.at[c, y, fields], gather.at[core, sp, fields], r_in.at[k, core, sp],
                (chip * 2 + c, y),
            )

    pl.when(has_prior)(lambda: arrived(c2in, r_c2))
    for s in range(2):
        spec[s, :, 2] = spec[s, :, 2] + c2in[s].reshape(spaces, part, n)
    exchange(0, pl.ds(0, 3))
    gather[core, sp] = spec[core, sp]
    for k, fields in ((0, pl.ds(0, 3)),):
        for d in yc:
            y, c = owner(d)
            arrived(gather.at[c, y, fields], r_in.at[k, c, y])

    m = n // 2
    power = pw[...]
    square = power * power
    columns = []
    for c in range(2):
        own = [gather[c, :, i].reshape(m, n) for i in range(3)]
        for i, field in ((0, own[2]), (1, own[0])):
            columns.append(jnp.concatenate([field, (DT * S[i][2]) * own[1]], axis=0))
    modes = left(mz, jnp.concatenate(columns, axis=1))
    d0 = [modes[:, 2 * c * n : (2 * c + 1) * n] for c in range(2)]
    d1 = [modes[:, (2 * c + 1) * n : (2 * c + 2) * n] for c in range(2)]
    e = [power * (power * d0[c] + d1[c]) for c in range(2)]
    e2[...] = square * e[0] + e[1]

    waits_for(1, chips_x - 1 - cx)
    for x in x_peers:
        send(e2, xin.at[cx], r_x.at[cx], (at(cz, x, core), sp))
    xin[cx] = e2[...]
    p4 = square * square
    p16 = p4
    for _ in range(chips_x - 1):
        p16 = p16 * p4
    for x in x_peers:
        arrived(xin.at[x], r_x.at[x])

    def add_chip(x, carry):
        running, ahead = carry
        return p4 * running + xin[x], p4 * ahead

    start = (jnp.zeros((m, n), jnp.float32), jnp.ones((m, n), jnp.float32))
    before, ahead = lax.fori_loop(0, cx, add_chip, start)
    total, _ = lax.fori_loop(cx, chips_x, add_chip, (before, ahead))
    waits_for(2, z_last - z_first)

    later = [(cz + d, at(jnp.minimum(cz + d, chips_z - 1), cx, core)) for d in range(1, half + 1)]

    @pl.when(~ends)
    def _():
        tot[...] = total

    for z, t in later[:-1]:
        send(tot, zin.at[cz - half_at], r_z.at[cz - half_at], (t, sp), ~ends & (z < z_last))

    @pl.when(half_at == 0)
    def _():
        zin[half] = jnp.zeros((m, n), jnp.float32)

    pl.when(half_at > 0)(lambda: arrived(zin.at[half], r_z.at[half]))

    def add_group(z, earlier):
        arrived(zin.at[z], r_z.at[z])
        return p16 * earlier + zin[z]

    earlier = lax.fori_loop(0, cz - half_at, add_group, zin[half])

    @pl.when(ends)
    def _():
        tot[...] = p16 * earlier + total

    for z, t in later:
        send(tot, zin.at[half], r_z.at[half], (t, sp), ends & (z < z_last))

    change = ahead * earlier + before
    changes = []
    for c in range(2):
        for source in (d0[c], d1[c]):
            change = power * (change + source)
            changes.append(change)
    at_planes = left(nz, jnp.concatenate(changes, axis=1))
    for c in range(2):
        for f in range(2):
            piece = at_planes[:, (2 * c + f) * n : (2 * c + f + 1) * n]
            fine[c, :, f] = piece.reshape(spaces, 2 * part, n)
    started = len(sends)
    for d in yc:
        y, c = owner(d)
        send(fine.at[c, y], fin.at[core, sp], r_f.at[core, sp], (chip * 2 + c, y))
    fin[core, sp] = fine[core, sp]
    finish(0, started)
    for d in yc:
        y, c = owner(d)
        arrived(fin.at[c, y], r_f.at[c, y])

    received = [fin[s, :, f].reshape(n, n) for f in range(2) for s in range(2)]
    wide = right(jnp.concatenate(received, axis=0), vy)
    for f in range(2):
        tall = []
        for s in range(2):
            rows_of = wide[(2 * f + s) * n : (2 * f + s + 1) * n]
            tall.append(jnp.concatenate([rows_of[:, :n], rows_of[:, n:]], axis=0))
        refined = left(vx, jnp.concatenate(tall, axis=1))
        for s in range(2):
            for z in range(4):
                piece = refined[z * n : (z + 1) * n, s * n : (s + 1) * n]
                swept = s1[s, z + 1] if f == 0 else s2[s, z]
                out[0, f, s, z] = swept + piece

    finish(started)


def local(shape, nodes, initial):
    count, spaces, chips_x, chips_z, n = shape
    consts = tables(n, spaces)
    m = n // 2
    part = m // spaces
    f32 = jnp.float32
    vmem, sem = pltpu.VMEM, pltpu.SemaphoreType.DMA
    n_sends = 4 + 3 + 4 + 2 + 1 + 3 * (2 * spaces - 1) + chips_x - 1 + chips_z - 1
    scratch = [
        vmem((3, 2, 6, n, n), f32),
        vmem((2, 6, n, n), f32),
        vmem((2, 4, n, n), f32),
        vmem((2, 6, n + 16, n), f32),
        vmem((4, 2, n, 2 * n), f32),
    ]
    scratch += [vmem(c.shape, jnp.bfloat16) for c in consts[:-1]]
    scratch += [
        vmem((m, n), f32),
        vmem((2, 2, n, n), f32),
        vmem((2, 2, n, n), f32),
        vmem((2, spaces, 3, part, n), f32),
        vmem((2, m, n), f32),
        vmem((2, m, n), f32),
        vmem((2, spaces, 3, part, n), f32),
        vmem((m, n), f32),
        vmem((chips_x, m, n), f32),
        vmem((m, n), f32),
        vmem((chips_z // 2 + 1, m, n), f32),
        vmem((2, spaces, 2, 2 * part, n), f32),
        vmem((2, spaces, 2, 2 * part, n), f32),
        sem((n_sends,)),
        sem((9,)),
        sem((3,)),
        sem((2, 2)),
        sem((2,)),
        sem((2,)),
        sem(()),
        sem((2, 2, spaces)),
        sem((chips_x,)),
        sem((chips_z // 2 + 1,)),
        sem((2, spaces)),
        pltpu.SemaphoreType.REGULAR((3,)),
    ]
    operands = [nodes, initial, *[jnp.asarray(c) for c in consts]]
    anywhere = pl.BlockSpec(memory_space=pl.ANY)
    return pl.pallas_call(
        functools.partial(kernel, shape),
        out_shape=jax.ShapeDtypeStruct((1, 2, 2, 4, n, n), f32),
        in_specs=[anywhere] * (2 + len(consts)),
        out_specs=pl.BlockSpec(memory_space=pltpu.VMEM),
        scratch_shapes=scratch,
        compiler_params=pltpu.CompilerParams(
            collective_id=0, has_side_effects=True, vmem_limit_bytes=40 << 20
        ),
        name="iteration",
    )(*[pltpu.with_memory_space_constraint(x, pltpu.HBM) for x in operands])


def solution(mesh):
    count, spaces = mesh.shape["tm"], mesh.shape["space"]
    chips_x = 4 if count == 64 else 2
    chips_z = count // (2 * chips_x)
    in_specs = (P("tm", None, None, "space", None, None), P(None, "space", None, None))
    out_specs = P("tm", None, None, "space", None, None)

    def run(nodes, initial):
        shape = (count, spaces, chips_x, chips_z, nodes.shape[-1])
        return jax.shard_map(
            functools.partial(local, shape),
            mesh=mesh, in_specs=in_specs, out_specs=out_specs, check_vma=False,
        )(nodes, initial)

    return run
```

```python
import functools
import math

import jax
import jax.numpy as jnp
import ml_dtypes
import numpy as np
from jax import lax
from jax.experimental import pallas as pl
from jax.experimental.pallas import tpu as pltpu
from jax.sharding import PartitionSpec as P

MESH = pl.DeviceIdType.MESH
DIFFUSE = (0.5, 0.25)
DECAY = (0.04, 0.1)
SIGN = (-1.0, 1.0)
DT = 0.5
H = 0.25
S = ((5.0 / 24.0, 1.0 / 3.0, -1.0 / 24.0), (-1.0 / 24.0, 1.0 / 3.0, 5.0 / 24.0))
ROWS = 32


def sine_table(points, modes, stretch):
    place = np.arange(points) + 0.5
    order = np.arange(modes) + 1.0
    angle = math.pi / (stretch * modes) * place[:, None] * order[None, :]
    weight = np.where(np.arange(modes) == modes - 1, math.sqrt(0.5), 1.0)
    return math.sqrt(2.0 / modes) * weight[None, :] * np.sin(angle)


def two_parts(table):
    high = table.astype(np.float32).astype(ml_dtypes.bfloat16)
    low = (table - high.astype(np.float64)).astype(np.float32).astype(ml_dtypes.bfloat16)
    return np.stack([high, low])


@functools.lru_cache(maxsize=None)
def tables(n, spaces):
    m, mz = n // 2, 2 * spaces
    half = m // 2
    per = half // spaces
    average = np.kron(np.eye(m), np.array([[0.5, 0.5]]))
    fine = sine_table(m, m, 1.0).T @ average
    fx = np.zeros((2, half, 2, 2, n))
    for z in range(2):
        fx[:, :, z, z, :] = 0.5 * fine.reshape(2, half, n)
    fx = fx.reshape(2 * m, 2 * n)
    fy = np.kron(np.eye(2), fine.T)
    wz = sine_table(mz, mz, 1.0).T
    own = np.zeros((mz, per, spaces, per, 2))
    edge = np.zeros((mz, per, spaces, per, 2))
    for i in range(per):
        for y in range(spaces):
            for z in range(2):
                own[:, i, y, i, z] = wz[:, 2 * y + z]
            if y > 0:
                edge[:, i, y, i, 0] = wz[:, 2 * y - 1]
            if y < spaces - 1:
                edge[:, i, y, i, 1] = wz[:, 2 * y + 2]
    own, edge = own.reshape(m, m), edge.reshape(m, m)
    mats = np.concatenate([own, edge], axis=1)
    nz = np.kron(sine_table(2 * mz, mz, 2.0), np.eye(per))
    vxy = sine_table(n, m, 2.0)
    vy = np.kron(np.eye(2), vxy.T)
    vx = np.zeros((4, n, 2, spaces, 4, per))
    for f in range(4):
        vx[f, :, :, :, f, :] = vxy.reshape(n, 2, spaces, per)
    vx = vx.reshape(4 * n, 2 * spaces * 4 * per)

    def eigen(modes):
        return 2.0 * np.cos(math.pi * (np.arange(modes) + 1.0) / modes) - 2.0

    ab = (eigen(m)[:, None] + eigen(m)[None, :]).reshape(2, spaces, per, m)
    e = (eigen(mz)[None, :, None, None, None] + ab.transpose(1, 2, 0, 3)[:, None]) / 4.0
    lin = np.stack([d * e - k for d, k in zip(DIFFUSE, DECAY)])
    factor = 1.0 / (1.0 - H * lin)
    factor = factor.reshape(2, spaces, m, n).astype(np.float32)
    return tuple(map(two_parts, (fx, fy, mats, nz, vy, vx))) + (factor,)


def split(x):
    high = x.astype(jnp.bfloat16)
    low = (x - high.astype(jnp.float32)).astype(jnp.bfloat16)
    return high, low


def dot(a, b):
    return jnp.dot(a, b, preferred_element_type=jnp.float32)


def left(table, x):
    high, low = split(x)
    return dot(table[0], high) + (dot(table[0], low) + dot(table[1], high))


def right(x, table):
    high, low = split(x)
    return dot(high, table[0]) + (dot(low, table[0]) + dot(high, table[1]))


def kernel(
    shape,
    nodes, initial, fx_h, fy_h, mz_h, nz_h, vy_h, vx_h, p_h,
    out,
    u, s1, s2, a, g, fx, fy, mz, nz, vy, vx, pw,
    sx, rim, spec, c2out, c2in, gather, e2, xin, tot, zin, fine, fin,
    ssem, lsem, r_u0, r_h, r_u0h, r_s1, r_c2, r_in, r_x, r_z, r_f, credit,
):
    count, spaces, chips_x, chips_z, n = shape
    tm, sp = lax.axis_index("tm"), lax.axis_index("space")
    core = lax.rem(tm, 2)
    chip = tm // 2
    cx, cz = lax.rem(chip, chips_x), chip // chips_x
    sends = []

    def at(z, x, c):
        return (z * chips_x + x) * 2 + c

    def send(src, dst, sem, device, when=None):
        copy = pltpu.make_async_remote_copy(
            src, dst, ssem.at[len(sends)], sem, device_id=device, device_id_type=MESH
        )
        sends.append((copy, when))
        if when is None:
            copy.start()
        else:
            pl.when(when)(copy.start)

    def finish(first, last=None):
        for copy, when in sends[first:last]:
            if when is None:
                copy.wait_send()
            else:
                pl.when(when)(copy.wait_send)

    def arrived(dst, sem):
        pltpu.make_async_copy(dst, dst, sem).wait()

    has_lo, has_hi = sp > 0, sp < spaces - 1
    lo, hi = (tm, jnp.maximum(sp - 1, 0)), (tm, jnp.minimum(sp + 1, spaces - 1))
    has_next, has_prior = tm < count - 1, tm > 0
    nxt = (lax.rem(tm + 1, count), sp)
    prv = (lax.rem(tm + count - 1, count), sp)
    ring = sorted(range(spaces), key=lambda d: -min(d, spaces - d))
    yc = [(d, c) for d in ring for c in (1, 0) if (d, c) != (0, 0)]

    def owner(d):
        return lax.rem(sp + d[0], spaces), lax.rem(core + d[1], 2)

    x_peers = [lax.rem(cx + d, chips_x) for d in (2, 1, 3) if d < chips_x]
    if chips_x == 2:
        x_peers = [1 - cx]

    loads = [
        pltpu.make_async_copy(nodes.at[0, 0], u.at[1, :, pl.ds(1, 4)], lsem.at[0]),
        pltpu.make_async_copy(nodes.at[0, 1], u.at[2, :, pl.ds(1, 4)], lsem.at[1]),
        pltpu.make_async_copy(fx_h, fx, lsem.at[2]),
        pltpu.make_async_copy(fy_h, fy, lsem.at[3]),
        pltpu.make_async_copy(mz_h, mz, lsem.at[4]),
        pltpu.make_async_copy(nz_h, nz, lsem.at[5]),
        pltpu.make_async_copy(vy_h, vy, lsem.at[6]),
        pltpu.make_async_copy(vx_h, vx, lsem.at[7]),
        pltpu.make_async_copy(p_h.at[core, sp], pw, lsem.at[8]),
    ]
    for load in loads:
        load.start()
    whole = pl.ds(1, 4)

    @pl.when(tm == 0)
    def _():
        pltpu.make_async_copy(initial, u.at[0, :, whole], r_u0).start()

    barrier = pltpu.get_barrier_semaphore()

    def one(flag):
        return jnp.where(flag, 1, 0)

    sibling = tm + 1 - 2 * core
    beside = lax.rem(tm + count - 1 + 2 * core, count)
    has_beside = jnp.where(core == 1, has_next, has_prior)

    half = chips_z // 2
    half_at = (cz // half) * half
    ends = cz == half_at + half - 1
    z_first = cz + 1
    z_last = jnp.where(ends, jnp.minimum(half_at + 2 * half, chips_z), half_at + half)
    z_below = cz - half_at + one(half_at > 0)

    def greet(t, y):
        pl.semaphore_signal(barrier, 1, device_id=(t, y), device_id_type=MESH)

    def answer(which, t, y):
        pl.semaphore_signal(credit.at[which], 1, device_id=(t, y), device_id_type=MESH)

    def waits_for(which, answers):
        pl.when(answers > 0)(lambda: pl.semaphore_wait(credit.at[which], answers))

    def over(lower, upper, work):
        def step(i, carry):
            work(i)
            return carry

        lax.fori_loop(lower, upper, step, 0)

    def far_columns(y, call):
        call(sibling, y)
        pl.when((y != sp + 1) & (y != sp - 1))(lambda: call(tm, y))

    pl.when(has_hi)(lambda: greet(tm, hi[1]))
    pl.when(has_lo)(lambda: greet(tm, lo[1]))
    greet(sibling, sp)
    pl.when(has_beside)(lambda: greet(beside, sp))
    over(sp + 1, spaces, lambda y: far_columns(y, greet))
    over(cx + 1, chips_x, lambda x: greet(at(cz, x, core), sp))
    over(z_first, z_last, lambda z: greet(at(z, cx, core), sp))

    below_far = 2 * sp - one(has_lo)
    above_far = 2 * (spaces - 1 - sp) - one(has_hi)
    pl.semaphore_wait(
        barrier,
        one(has_lo) + one(has_hi) + 1 + one(has_beside)
        + below_far + cx + z_below,
    )

    send(nodes.at[0, 1], u.at[0, :, whole], r_u0, nxt, has_next)
    for node in (2, 1):
        send(nodes.at[0, node - 1, :, 3], u.at[node, :, 0], r_h.at[node - 1, 0], hi, has_hi)
        send(nodes.at[0, node - 1, :, 0], u.at[node, :, 5], r_h.at[node - 1, 1], lo, has_lo)
    over(0, sp, lambda y: far_columns(y, functools.partial(answer, 0)))
    over(0, cx, lambda x: answer(1, at(cz, x, core), sp))
    over(half_at, cz, lambda z: answer(2, at(z, cx, core), sp))
    pl.when(half_at > 0)(lambda: answer(2, at(half_at - 1, cx, core), sp))

    zero = jnp.zeros((n, n), jnp.float32)
    for s in range(2):
        for z in range(6):
            a[s, z, 0:8, :] = jnp.zeros((8, n), jnp.float32)
            a[s, z, 8 + n : 16 + n, :] = jnp.zeros((8, n), jnp.float32)

    def outside(plane):
        for s in range(2):
            for i in range(3):
                u[i, s, plane] = zero
            s1[s, plane] = zero

    pl.when(sp == 0)(lambda: outside(0))
    pl.when(sp == spaces - 1)(lambda: outside(5))

    @pl.when(tm == 0)
    def _():
        c2in[...] = jnp.zeros(c2in.shape, jnp.float32)

    lane = lax.broadcasted_iota(jnp.int32, (ROWS, n), 1)
    first_lane, last_lane = lane == 0, lane == n - 1
    chunks = range(0, n, ROWS)

    def react(p, q):
        return (1.0 + p) * (q * q)

    def sides(s, z, r):
        mid = a[s, z, 8 + r : 8 + r + ROWS, :]
        west = jnp.where(first_lane, 0.0, pltpu.roll(mid, 1, 1))
        east = jnp.where(last_lane, 0.0, pltpu.roll(mid, n - 1, 1))
        north = a[s, z, 7 + r : 7 + r + ROWS, :]
        south = a[s, z, 9 + r : 9 + r + ROWS, :]
        return (west + east) + (north + south), mid

    def rows(ref, *index, r):
        return ref[(*index, slice(r, r + ROWS), slice(None))]

    def sum_one(z, base=True):
        for r in chunks:
            pq = [[rows(u, i, s, z, r=r) for s in range(2)] for i in range(3)]
            if base:
                w = sum((DT * S[0][i]) * react(*pq[i]) for i in range(3))
            for s in range(2):
                total = sum((DT * S[0][i]) * pq[i][s] for i in range(3))
                a[s, z, 8 + r : 8 + r + ROWS, :] = total
                if base:
                    s1[s, z, r : r + ROWS, :] = pq[0][s] + SIGN[s] * w - DECAY[s] * total

    def sum_two(z, base=True):
        weight = (DT * S[1][0], DT * S[1][1] - H, DT * S[1][2])
        for r in chunks:
            pq = [[rows(u, i, s, z, r=r) for s in range(2)] for i in range(3)]
            ab = [rows(s1, s, z, r=r) for s in range(2)]
            if base:
                w = H * react(*ab) + sum(weight[i] * react(*pq[i]) for i in range(3))
            for s in range(2):
                total = H * ab[s] + sum(weight[i] * pq[i][s] for i in range(3))
                a[s, z, 8 + r : 8 + r + ROWS, :] = total
                if base:
                    s2[s, z - 1, r : r + ROWS, :] = ab[s] + SIGN[s] * w - DECAY[s] * total

    def diffuse(ref, z, shift):
        for r in chunks:
            for s in range(2):
                around, mid = sides(s, z, r)
                below = a[s, z - 1, 8 + r : 8 + r + ROWS, :]
                above = a[s, z + 1, 8 + r : 8 + r + ROWS, :]
                lap = around + (below + above) - 6.0 * mid
                ref[s, z - shift, r : r + ROWS, :] = (
                    ref[s, z - shift, r : r + ROWS, :] + DIFFUSE[s] * lap
                )

    loads[0].wait()
    loads[1].wait()
    pl.when(has_lo)(lambda: arrived(u.at[2, :, 0], r_h.at[1, 0]))
    pl.when(has_hi)(lambda: arrived(u.at[2, :, 5], r_h.at[1, 1]))
    send(u.at[2, :, 0], u.at[0, :, 0], r_u0h.at[0], nxt, has_lo & has_next)
    send(u.at[2, :, 5], u.at[0, :, 5], r_u0h.at[1], nxt, has_hi & has_next)
    arrived(u.at[0, :, whole], r_u0)
    send(u.at[0, :, 4], u.at[0, :, 0], r_u0h.at[0], hi, has_hi & ~has_prior)
    send(u.at[0, :, 1], u.at[0, :, 5], r_u0h.at[1], lo, has_lo & ~has_prior)
    for z in (1, 2, 3, 4):
        sum_one(z)
    edges = ((0, 1, 2, 0), (1, 4, 3, 5))
    for k, z, inner, _ in edges:
        for r in chunks:
            for s in range(2):
                around, mid = sides(s, z, r)
                lap = around + a[s, inner, 8 + r : 8 + r + ROWS, :] - 6.0 * mid
                sx[k, s, r : r + ROWS, :] = rows(s1, s, z, r=r) + DIFFUSE[s] * lap
                rim[k, s, r : r + ROWS, :] = DIFFUSE[s] * mid
        if k == 0:
            send(sx.at[0], s1.at[:, 5], r_s1.at[1], lo, has_lo)
        else:
            send(sx.at[1], s1.at[:, 0], r_s1.at[0], hi, has_hi)
    for z in (2, 3):
        diffuse(s1, z, 0)
    for k, z, _, outer in edges:
        has = (has_lo, has_hi)[k]
        ready = [(u.at[1, :, outer], r_h.at[0, k]), (u.at[0, :, outer], r_u0h.at[k])]
        for dst, landed in ready:
            pl.when(has)(functools.partial(arrived, dst, landed))
        sum_one(outer, False)
        for r in chunks:
            for s in range(2):
                beyond = a[s, outer, 8 + r : 8 + r + ROWS, :]
                s1[s, z, r : r + ROWS, :] = sx[k, s, r : r + ROWS, :] + DIFFUSE[s] * beyond

    for z in (1, 2, 3, 4):
        sum_two(z)
    for z in (2, 3):
        diffuse(s2, z, 1)

    def complete(k, outer):
        arrived(s1.at[:, outer], r_s1.at[k])
        for r in chunks:
            for s in range(2):
                s1[s, outer, r : r + ROWS, :] = rows(s1, s, outer, r=r) + rim[k, s, r : r + ROWS, :]

    pl.when(has_lo)(lambda: complete(0, 0))
    sum_two(0, False)
    pl.when(has_hi)(lambda: complete(1, 5))
    sum_two(5, False)
    diffuse(s2, 1, 1)
    diffuse(s2, 4, 1)

    for load in loads[2:]:
        load.wait()

    def to_modes(fields):
        both = [jnp.concatenate([g[i, 0], g[i, 1]], axis=0) for i in fields]
        along_x = left(fx, jnp.concatenate(both, axis=1))
        half_rows = n // 2
        wide = jnp.concatenate(
            [
                jnp.concatenate(
                    [along_x[:half_rows, k * n : (k + 1) * n], along_x[half_rows:, k * n : (k + 1) * n]],
                    axis=1,
                )
                for k in range(2 * len(fields))
            ],
            axis=0,
        )
        modes = right(wide, fy)
        return [modes[k * half_rows : (k + 1) * half_rows] for k in range(2 * len(fields))]

    part = n // 2 // spaces
    for j in range(2):
        for r in chunks:
            for s in range(2):
                at_s = slice(s * n, (s + 1) * n)
                g[3, j, r : r + ROWS, at_s] = rows(s2, s, 2 * j, r=r) + rows(s2, s, 2 * j + 1, r=r)
    ends_modes = to_modes([3])
    for s in range(2):
        c2out[s] = ends_modes[s]
    send(c2out, c2in, r_c2, nxt, has_next)
    is_first = jnp.where(tm == 0, 1.0, 0.0)
    for i in range(2):
        for j in range(2):
            z = 2 * j + 1
            for r in chunks:
                w = 0.0
                both = [0.0, 0.0]
                keep = [0.0, 0.0]
                for k in (z, z + 1):
                    p0 = [rows(u, 0, s, k, r=r) for s in range(2)]
                    p1 = [rows(s1, s, k, r=r) for s in range(2)]
                    p2 = [rows(s2, s, k - 1, r=r) for s in range(2)]
                    three = (p0, p1, p2)
                    w = w + sum((DT * S[i][t]) * react(*three[t]) for t in range(3))
                    for s in range(2):
                        total = sum((DT * S[i][t]) * three[t][s] for t in range(3))
                        both[s] = both[s] + total
                        if i == 0:
                            keep[s] = keep[s] + is_first * p0[s] - p1[s]
                        else:
                            keep[s] = keep[s] + p1[s] - p2[s]
                for s in range(2):
                    out_of = 0 if j == 0 else 5
                    near = 3 if j == 0 else 2
                    beyond = (DT * S[i][0]) * rows(u, 0, s, out_of, r=r) + (DT * S[i][1]) * rows(
                        s1, s, out_of, r=r
                    )
                    beyond = beyond + (
                        (DT * S[i][0]) * rows(u, 0, s, near, r=r)
                        + (DT * S[i][1]) * rows(s1, s, near, r=r)
                        + (DT * S[i][2]) * rows(s2, s, near - 1, r=r)
                    )
                    a[s, j, 8 + r : 8 + r + ROWS, :] = both[s]
                    g[i, j, r : r + ROWS, s * n : (s + 1) * n] = (
                        keep[s]
                        + SIGN[s] * w
                        - DECAY[s] * both[s]
                        + DIFFUSE[s] * (beyond - 5.0 * both[s])
                    )
            for r in chunks:
                for s in range(2):
                    around, _ = sides(s, j, r)
                    at_s = slice(s * n, (s + 1) * n)
                    g[i, j, r : r + ROWS, at_s] = (
                        g[i, j, r : r + ROWS, at_s] + DIFFUSE[s] * around
                    )
    for j in range(2):
        for r in chunks:
            for s in range(2):
                at_s = slice(s * n, (s + 1) * n)
                g[2, j, r : r + ROWS, at_s] = DIFFUSE[s] * rows(s2, s, 3 * j, r=r)

    others = to_modes([1, 2, 0])
    for i in range(3):
        for s in range(2):
            spec[s, :, i] = others[2 * i + s].reshape(spaces, part, n)
    waits_for(0, above_far)

    def exchange(k, fields):
        for d in yc:
            y, c = owner(d)
            send(
                spec.at[c, y, fields], gather.at[core, sp, fields], r_in.at[k, core, sp],
                (chip * 2 + c, y),
            )

    pl.when(has_prior)(lambda: arrived(c2in, r_c2))
    for s in range(2):
        spec[s, :, 2] = spec[s, :, 2] + c2in[s].reshape(spaces, part, n)
    exchange(0, pl.ds(0, 3))
    gather[core, sp] = spec[core, sp]
    for k, fields in ((0, pl.ds(0, 3)),):
        for d in yc:
            y, c = owner(d)
            arrived(gather.at[c, y, fields], r_in.at[k, c, y])

    m = n // 2
    power = pw[...]
    square = power * power
    columns = []
    for c in range(2):
        own = [gather[c, :, i].reshape(m, n) for i in range(3)]
        for i, field in ((0, own[2]), (1, own[0])):
            columns.append(jnp.concatenate([field, (DT * S[i][2]) * own[1]], axis=0))
    modes = left(mz, jnp.concatenate(columns, axis=1))
    d0 = [modes[:, 2 * c * n : (2 * c + 1) * n] for c in range(2)]
    d1 = [modes[:, (2 * c + 1) * n : (2 * c + 2) * n] for c in range(2)]
    e = [power * (power * d0[c] + d1[c]) for c in range(2)]
    e2[...] = square * e[0] + e[1]

    waits_for(1, chips_x - 1 - cx)
    for x in x_peers:
        send(e2, xin.at[cx], r_x.at[cx], (at(cz, x, core), sp))
    xin[cx] = e2[...]
    p4 = square * square
    p16 = p4
    for _ in range(chips_x - 1):
        p16 = p16 * p4
    for x in x_peers:
        arrived(xin.at[x], r_x.at[x])

    def add_chip(x, carry):
        running, ahead = carry
        return p4 * running + xin[x], p4 * ahead

    start = (jnp.zeros((m, n), jnp.float32), jnp.ones((m, n), jnp.float32))
    before, ahead = lax.fori_loop(0, cx, add_chip, start)
    total, _ = lax.fori_loop(cx, chips_x, add_chip, (before, ahead))
    waits_for(2, z_last - z_first)

    later = [(cz + d, at(jnp.minimum(cz + d, chips_z - 1), cx, core)) for d in range(1, half + 1)]

    @pl.when(~ends)
    def _():
        tot[...] = total

    for z, t in later[:-1]:
        send(tot, zin.at[cz - half_at], r_z.at[cz - half_at], (t, sp), ~ends & (z < z_last))

    @pl.when(half_at == 0)
    def _():
        zin[half] = jnp.zeros((m, n), jnp.float32)

    pl.when(half_at > 0)(lambda: arrived(zin.at[half], r_z.at[half]))

    def add_group(z, earlier):
        arrived(zin.at[z], r_z.at[z])
        return p16 * earlier + zin[z]

    earlier = lax.fori_loop(0, cz - half_at, add_group, zin[half])

    @pl.when(ends)
    def _():
        tot[...] = p16 * earlier + total

    for z, t in later:
        send(tot, zin.at[half], r_z.at[half], (t, sp), ends & (z < z_last))

    change = ahead * earlier + before
    changes = []
    for c in range(2):
        for source in (d0[c], d1[c]):
            change = power * (change + source)
            changes.append(change)
    at_planes = left(nz, jnp.concatenate(changes, axis=1))
    for c in range(2):
        for f in range(2):
            piece = at_planes[:, (2 * c + f) * n : (2 * c + f + 1) * n]
            fine[c, :, f] = piece.reshape(spaces, 2 * part, n)
    started = len(sends)
    for d in yc:
        y, c = owner(d)
        send(fine.at[c, y], fin.at[core, sp], r_f.at[core, sp], (chip * 2 + c, y))
    fin[core, sp] = fine[core, sp]
    finish(0, started)
    for d in yc:
        y, c = owner(d)
        arrived(fin.at[c, y], r_f.at[c, y])

    received = [fin[s, :, f].reshape(n, n) for f in range(2) for s in range(2)]
    wide = right(jnp.concatenate(received, axis=0), vy)
    for f in range(2):
        tall = []
        for s in range(2):
            rows_of = wide[(2 * f + s) * n : (2 * f + s + 1) * n]
            tall.append(jnp.concatenate([rows_of[:, :n], rows_of[:, n:]], axis=0))
        refined = left(vx, jnp.concatenate(tall, axis=1))
        for s in range(2):
            for z in range(4):
                piece = refined[z * n : (z + 1) * n, s * n : (s + 1) * n]
                swept = s1[s, z + 1] if f == 0 else s2[s, z]
                out[0, f, s, z] = swept + piece

    finish(started)


def local(shape, nodes, initial):
    count, spaces, chips_x, chips_z, n = shape
    consts = tables(n, spaces)
    m = n // 2
    part = m // spaces
    f32 = jnp.float32
    vmem, sem = pltpu.VMEM, pltpu.SemaphoreType.DMA
    n_sends = 4 + 1 + 4 + 2 + 1 + 3 * (2 * spaces - 1) + chips_x - 1 + chips_z - 1
    scratch = [
        vmem((3, 2, 6, n, n), f32),
        vmem((2, 6, n, n), f32),
        vmem((2, 4, n, n), f32),
        vmem((2, 6, n + 16, n), f32),
        vmem((4, 2, n, 2 * n), f32),
    ]
    scratch += [vmem(c.shape, jnp.bfloat16) for c in consts[:-1]]
    scratch += [
        vmem((m, n), f32),
        vmem((2, 2, n, n), f32),
        vmem((2, 2, n, n), f32),
        vmem((2, spaces, 3, part, n), f32),
        vmem((2, m, n), f32),
        vmem((2, m, n), f32),
        vmem((2, spaces, 3, part, n), f32),
        vmem((m, n), f32),
        vmem((chips_x, m, n), f32),
        vmem((m, n), f32),
        vmem((chips_z // 2 + 1, m, n), f32),
        vmem((2, spaces, 2, 2 * part, n), f32),
        vmem((2, spaces, 2, 2 * part, n), f32),
        sem((n_sends,)),
        sem((9,)),
        sem(()),
        sem((2, 2)),
        sem((2,)),
        sem((2,)),
        sem(()),
        sem((2, 2, spaces)),
        sem((chips_x,)),
        sem((chips_z // 2 + 1,)),
        sem((2, spaces)),
        pltpu.SemaphoreType.REGULAR((3,)),
    ]
    operands = [nodes, initial, *[jnp.asarray(c) for c in consts]]
    anywhere = pl.BlockSpec(memory_space=pl.ANY)
    return pl.pallas_call(
        functools.partial(kernel, shape),
        out_shape=jax.ShapeDtypeStruct((1, 2, 2, 4, n, n), f32),
        in_specs=[anywhere] * (2 + len(consts)),
        out_specs=pl.BlockSpec(memory_space=pltpu.VMEM),
        scratch_shapes=scratch,
        compiler_params=pltpu.CompilerParams(
            collective_id=0, has_side_effects=True, vmem_limit_bytes=40 << 20
        ),
        name="iteration",
    )(*[pltpu.with_memory_space_constraint(x, pltpu.HBM) for x in operands])


def solution(mesh):
    count, spaces = mesh.shape["tm"], mesh.shape["space"]
    chips_x = 4 if count == 64 else 2
    chips_z = count // (2 * chips_x)
    in_specs = (P("tm", None, None, "space", None, None), P(None, "space", None, None))
    out_specs = P("tm", None, None, "space", None, None)

    def run(nodes, initial):
        shape = (count, spaces, chips_x, chips_z, nodes.shape[-1])
        return jax.shard_map(
            functools.partial(local, shape),
            mesh=mesh, in_specs=in_specs, out_specs=out_specs, check_vma=False,
        )(nodes, initial)

    return run
```

```python
import functools
import math

import jax
import jax.numpy as jnp
import ml_dtypes
import numpy as np
from jax import lax
from jax.experimental import pallas as pl
from jax.experimental.pallas import tpu as pltpu
from jax.sharding import PartitionSpec as P

MESH = pl.DeviceIdType.MESH
DIFFUSE = (0.5, 0.25)
DECAY = (0.04, 0.1)
SIGN = (-1.0, 1.0)
DT = 0.5
H = 0.25
S = ((5.0 / 24.0, 1.0 / 3.0, -1.0 / 24.0), (-1.0 / 24.0, 1.0 / 3.0, 5.0 / 24.0))
ROWS = 32


def sine_table(points, modes, stretch):
    place = np.arange(points) + 0.5
    order = np.arange(modes) + 1.0
    angle = math.pi / (stretch * modes) * place[:, None] * order[None, :]
    weight = np.where(np.arange(modes) == modes - 1, math.sqrt(0.5), 1.0)
    return math.sqrt(2.0 / modes) * weight[None, :] * np.sin(angle)


def two_parts(table):
    high = table.astype(np.float32).astype(ml_dtypes.bfloat16)
    low = (table - high.astype(np.float64)).astype(np.float32).astype(ml_dtypes.bfloat16)
    return np.stack([high, low])


@functools.lru_cache(maxsize=None)
def tables(n, spaces):
    m, mz = n // 2, 2 * spaces
    half = m // 2
    per = half // spaces
    average = np.kron(np.eye(m), np.array([[0.5, 0.5]]))
    fine = sine_table(m, m, 1.0).T @ average
    fx = np.zeros((2, half, 2, 2, n))
    for z in range(2):
        fx[:, :, z, z, :] = 0.5 * fine.reshape(2, half, n)
    fx = fx.reshape(2 * m, 2 * n)
    fy = np.kron(np.eye(2), fine.T)
    wz = sine_table(mz, mz, 1.0).T
    own = np.zeros((mz, per, spaces, per, 2))
    edge = np.zeros((mz, per, spaces, per, 2))
    for i in range(per):
        for y in range(spaces):
            for z in range(2):
                own[:, i, y, i, z] = wz[:, 2 * y + z]
            if y > 0:
                edge[:, i, y, i, 0] = wz[:, 2 * y - 1]
            if y < spaces - 1:
                edge[:, i, y, i, 1] = wz[:, 2 * y + 2]
    own, edge = own.reshape(m, m), edge.reshape(m, m)
    mats = np.concatenate([own, edge], axis=1)
    nz = np.kron(sine_table(2 * mz, mz, 2.0), np.eye(per))
    vxy = sine_table(n, m, 2.0)
    vy = np.kron(np.eye(2), vxy.T)
    vx = np.zeros((4, n, 2, spaces, 4, per))
    for f in range(4):
        vx[f, :, :, :, f, :] = vxy.reshape(n, 2, spaces, per)
    vx = vx.reshape(4 * n, 2 * spaces * 4 * per)

    def eigen(modes):
        return 2.0 * np.cos(math.pi * (np.arange(modes) + 1.0) / modes) - 2.0

    ab = (eigen(m)[:, None] + eigen(m)[None, :]).reshape(2, spaces, per, m)
    e = (eigen(mz)[None, :, None, None, None] + ab.transpose(1, 2, 0, 3)[:, None]) / 4.0
    lin = np.stack([d * e - k for d, k in zip(DIFFUSE, DECAY)])
    factor = 1.0 / (1.0 - H * lin)
    factor = factor.reshape(2, spaces, m, n).astype(np.float32)
    return tuple(map(two_parts, (fx, fy, mats, nz, vy, vx))) + (factor,)


def split(x):
    high = x.astype(jnp.bfloat16)
    low = (x - high.astype(jnp.float32)).astype(jnp.bfloat16)
    return high, low


def dot(a, b):
    return jnp.dot(a, b, preferred_element_type=jnp.float32)


def left(table, x):
    high, low = split(x)
    return dot(table[0], high) + (dot(table[0], low) + dot(table[1], high))


def right(x, table):
    high, low = split(x)
    return dot(high, table[0]) + (dot(low, table[0]) + dot(high, table[1]))


def kernel(
    shape,
    nodes, initial, fx_h, fy_h, mz_h, nz_h, vy_h, vx_h, p_h,
    out,
    u, s1, s2, a, g, fx, fy, mz, nz, vy, vx, pw,
    sx, rim, spec, c2out, c2in, gather, e2, xin, tot, zin, fine, fin,
    ssem, lsem, r_u0, r_h, r_u0h, r_s1, r_c2, r_in, r_x, r_z, r_f, credit,
):
    count, spaces, chips_x, chips_z, n = shape
    tm, sp = lax.axis_index("tm"), lax.axis_index("space")
    core = lax.rem(tm, 2)
    chip = tm // 2
    cx, cz = lax.rem(chip, chips_x), chip // chips_x
    sends = []

    def at(z, x, c):
        return (z * chips_x + x) * 2 + c

    def send(src, dst, sem, device, when=None):
        copy = pltpu.make_async_remote_copy(
            src, dst, ssem.at[len(sends)], sem, device_id=device, device_id_type=MESH
        )
        sends.append((copy, when))
        if when is None:
            copy.start()
        else:
            pl.when(when)(copy.start)

    def finish(first, last=None):
        for copy, when in sends[first:last]:
            if when is None:
                copy.wait_send()
            else:
                pl.when(when)(copy.wait_send)

    def arrived(dst, sem):
        pltpu.make_async_copy(dst, dst, sem).wait()

    has_lo, has_hi = sp > 0, sp < spaces - 1
    lo, hi = (tm, jnp.maximum(sp - 1, 0)), (tm, jnp.minimum(sp + 1, spaces - 1))
    has_next, has_prior = tm < count - 1, tm > 0
    nxt = (lax.rem(tm + 1, count), sp)
    prv = (lax.rem(tm + count - 1, count), sp)
    ring = sorted(range(spaces), key=lambda d: -min(d, spaces - d))
    yc = [(d, c) for d in ring for c in (1, 0) if (d, c) != (0, 0)]

    def owner(d):
        return lax.rem(sp + d[0], spaces), lax.rem(core + d[1], 2)

    x_peers = [lax.rem(cx + d, chips_x) for d in (2, 1, 3) if d < chips_x]
    if chips_x == 2:
        x_peers = [1 - cx]

    loads = [
        pltpu.make_async_copy(nodes.at[0, 0], u.at[1, :, pl.ds(1, 4)], lsem.at[0]),
        pltpu.make_async_copy(nodes.at[0, 1], u.at[2, :, pl.ds(1, 4)], lsem.at[1]),
        pltpu.make_async_copy(fx_h, fx, lsem.at[2]),
        pltpu.make_async_copy(fy_h, fy, lsem.at[3]),
        pltpu.make_async_copy(mz_h, mz, lsem.at[4]),
        pltpu.make_async_copy(nz_h, nz, lsem.at[5]),
        pltpu.make_async_copy(vy_h, vy, lsem.at[6]),
        pltpu.make_async_copy(vx_h, vx, lsem.at[7]),
        pltpu.make_async_copy(p_h.at[core, sp], pw, lsem.at[8]),
    ]
    for load in loads:
        load.start()
    whole = pl.ds(1, 4)

    @pl.when(tm == 0)
    def _():
        pltpu.make_async_copy(initial, u.at[0, :, whole], r_u0).start()

    barrier = pltpu.get_barrier_semaphore()

    def one(flag):
        return jnp.where(flag, 1, 0)

    sibling = tm + 1 - 2 * core
    beside = lax.rem(tm + count - 1 + 2 * core, count)
    has_beside = jnp.where(core == 1, has_next, has_prior)

    half = chips_z // 2
    half_at = (cz // half) * half
    ends = cz == half_at + half - 1
    z_first = cz + 1
    z_last = jnp.where(ends, jnp.minimum(half_at + 2 * half, chips_z), half_at + half)
    z_below = cz - half_at + one(half_at > 0)

    def greet(t, y):
        pl.semaphore_signal(barrier, 1, device_id=(t, y), device_id_type=MESH)

    def answer(which, t, y):
        pl.semaphore_signal(credit.at[which], 1, device_id=(t, y), device_id_type=MESH)

    def waits_for(which, answers):
        pl.when(answers > 0)(lambda: pl.semaphore_wait(credit.at[which], answers))

    def over(lower, upper, work):
        def step(i, carry):
            work(i)
            return carry

        lax.fori_loop(lower, upper, step, 0)

    def far_columns(y, call):
        call(sibling, y)
        pl.when((y != sp + 1) & (y != sp - 1))(lambda: call(tm, y))

    pl.when(has_hi)(lambda: greet(tm, hi[1]))
    pl.when(has_lo)(lambda: greet(tm, lo[1]))
    greet(sibling, sp)
    pl.when(has_beside)(lambda: greet(beside, sp))
    over(sp + 1, spaces, lambda y: far_columns(y, greet))
    over(cx + 1, chips_x, lambda x: greet(at(cz, x, core), sp))
    over(z_first, z_last, lambda z: greet(at(z, cx, core), sp))

    below_far = 2 * sp - one(has_lo)
    above_far = 2 * (spaces - 1 - sp) - one(has_hi)
    pl.semaphore_wait(
        barrier,
        one(has_lo) + one(has_hi) + 1 + one(has_beside)
        + below_far + cx + z_below,
    )

    send(nodes.at[0, 1], u.at[0, :, whole], r_u0, nxt, has_next)
    for node in (2, 1):
        send(nodes.at[0, node - 1, :, 3], u.at[node, :, 0], r_h.at[node - 1, 0], hi, has_hi)
        send(nodes.at[0, node - 1, :, 0], u.at[node, :, 5], r_h.at[node - 1, 1], lo, has_lo)
    over(0, sp, lambda y: far_columns(y, functools.partial(answer, 0)))
    over(0, cx, lambda x: answer(1, at(cz, x, core), sp))
    over(half_at, cz, lambda z: answer(2, at(z, cx, core), sp))
    pl.when(half_at > 0)(lambda: answer(2, at(half_at - 1, cx, core), sp))

    zero = jnp.zeros((n, n), jnp.float32)
    for s in range(2):
        for z in range(6):
            a[s, z, 0:8, :] = jnp.zeros((8, n), jnp.float32)
            a[s, z, 8 + n : 16 + n, :] = jnp.zeros((8, n), jnp.float32)

    def outside(plane):
        for s in range(2):
            for i in range(3):
                u[i, s, plane] = zero
            s1[s, plane] = zero

    pl.when(sp == 0)(lambda: outside(0))
    pl.when(sp == spaces - 1)(lambda: outside(5))

    @pl.when(tm == 0)
    def _():
        c2in[...] = jnp.zeros(c2in.shape, jnp.float32)

    lane = lax.broadcasted_iota(jnp.int32, (ROWS, n), 1)
    first_lane, last_lane = lane == 0, lane == n - 1
    chunks = range(0, n, ROWS)

    def react(p, q):
        return (1.0 + p) * (q * q)

    def sides(s, z, r):
        mid = a[s, z, 8 + r : 8 + r + ROWS, :]
        west = jnp.where(first_lane, 0.0, pltpu.roll(mid, 1, 1))
        east = jnp.where(last_lane, 0.0, pltpu.roll(mid, n - 1, 1))
        north = a[s, z, 7 + r : 7 + r + ROWS, :]
        south = a[s, z, 9 + r : 9 + r + ROWS, :]
        return (west + east) + (north + south), mid

    def rows(ref, *index, r):
        return ref[(*index, slice(r, r + ROWS), slice(None))]

    def sum_one(z, base=True):
        for r in chunks:
            pq = [[rows(u, i, s, z, r=r) for s in range(2)] for i in range(3)]
            if base:
                w = sum((DT * S[0][i]) * react(*pq[i]) for i in range(3))
            for s in range(2):
                total = sum((DT * S[0][i]) * pq[i][s] for i in range(3))
                a[s, z, 8 + r : 8 + r + ROWS, :] = total
                if base:
                    s1[s, z, r : r + ROWS, :] = pq[0][s] + SIGN[s] * w - DECAY[s] * total

    def begin_one(z):
        for r in chunks:
            pq = [[rows(u, i, s, z, r=r) for s in range(2)] for i in (1, 2)]
            w = sum((DT * S[0][i + 1]) * react(*pq[i]) for i in range(2))
            for s in range(2):
                total = sum((DT * S[0][i + 1]) * pq[i][s] for i in range(2))
                a[s, z, 8 + r : 8 + r + ROWS, :] = total
                s1[s, z, r : r + ROWS, :] = SIGN[s] * w - DECAY[s] * total

    def end_one(z):
        weight = DT * S[0][0]
        for r in chunks:
            pq = [rows(u, 0, s, z, r=r) for s in range(2)]
            w = weight * react(*pq)
            for s in range(2):
                own = weight * pq[s]
                at_r = slice(8 + r, 8 + r + ROWS)
                a[s, z, at_r, :] = a[s, z, at_r, :] + own
                s1[s, z, r : r + ROWS, :] = rows(s1, s, z, r=r) + (
                    pq[s] + SIGN[s] * w - DECAY[s] * own
                )

    def sum_two(z, base=True):
        weight = (DT * S[1][0], DT * S[1][1] - H, DT * S[1][2])
        for r in chunks:
            pq = [[rows(u, i, s, z, r=r) for s in range(2)] for i in range(3)]
            ab = [rows(s1, s, z, r=r) for s in range(2)]
            if base:
                w = H * react(*ab) + sum(weight[i] * react(*pq[i]) for i in range(3))
            for s in range(2):
                total = H * ab[s] + sum(weight[i] * pq[i][s] for i in range(3))
                a[s, z, 8 + r : 8 + r + ROWS, :] = total
                if base:
                    s2[s, z - 1, r : r + ROWS, :] = ab[s] + SIGN[s] * w - DECAY[s] * total

    def diffuse(ref, z, shift):
        for r in chunks:
            for s in range(2):
                around, mid = sides(s, z, r)
                below = a[s, z - 1, 8 + r : 8 + r + ROWS, :]
                above = a[s, z + 1, 8 + r : 8 + r + ROWS, :]
                lap = around + (below + above) - 6.0 * mid
                ref[s, z - shift, r : r + ROWS, :] = (
                    ref[s, z - shift, r : r + ROWS, :] + DIFFUSE[s] * lap
                )

    loads[0].wait()
    loads[1].wait()
    for z in (1, 2, 3, 4):
        begin_one(z)
    pl.when(has_lo)(lambda: arrived(u.at[2, :, 0], r_h.at[1, 0]))
    pl.when(has_hi)(lambda: arrived(u.at[2, :, 5], r_h.at[1, 1]))
    send(u.at[2, :, 0], u.at[0, :, 0], r_u0h.at[0], nxt, has_lo & has_next)
    send(u.at[2, :, 5], u.at[0, :, 5], r_u0h.at[1], nxt, has_hi & has_next)
    arrived(u.at[0, :, whole], r_u0)
    send(u.at[0, :, 4], u.at[0, :, 0], r_u0h.at[0], hi, has_hi & ~has_prior)
    send(u.at[0, :, 1], u.at[0, :, 5], r_u0h.at[1], lo, has_lo & ~has_prior)
    for z in (1, 2, 3, 4):
        end_one(z)
    edges = ((0, 1, 2, 0), (1, 4, 3, 5))
    for k, z, inner, _ in edges:
        for r in chunks:
            for s in range(2):
                around, mid = sides(s, z, r)
                lap = around + a[s, inner, 8 + r : 8 + r + ROWS, :] - 6.0 * mid
                sx[k, s, r : r + ROWS, :] = rows(s1, s, z, r=r) + DIFFUSE[s] * lap
                rim[k, s, r : r + ROWS, :] = DIFFUSE[s] * mid
        if k == 0:
            send(sx.at[0], s1.at[:, 5], r_s1.at[1], lo, has_lo)
        else:
            send(sx.at[1], s1.at[:, 0], r_s1.at[0], hi, has_hi)
    for z in (2, 3):
        diffuse(s1, z, 0)
    for k, z, _, outer in edges:
        has = (has_lo, has_hi)[k]
        ready = [(u.at[1, :, outer], r_h.at[0, k]), (u.at[0, :, outer], r_u0h.at[k])]
        for dst, landed in ready:
            pl.when(has)(functools.partial(arrived, dst, landed))
        sum_one(outer, False)
        for r in chunks:
            for s in range(2):
                beyond = a[s, outer, 8 + r : 8 + r + ROWS, :]
                s1[s, z, r : r + ROWS, :] = sx[k, s, r : r + ROWS, :] + DIFFUSE[s] * beyond

    for z in (1, 2, 3, 4):
        sum_two(z)
    for z in (2, 3):
        diffuse(s2, z, 1)

    def complete(k, outer):
        arrived(s1.at[:, outer], r_s1.at[k])
        for r in chunks:
            for s in range(2):
                s1[s, outer, r : r + ROWS, :] = rows(s1, s, outer, r=r) + rim[k, s, r : r + ROWS, :]

    pl.when(has_lo)(lambda: complete(0, 0))
    sum_two(0, False)
    pl.when(has_hi)(lambda: complete(1, 5))
    sum_two(5, False)
    diffuse(s2, 1, 1)
    diffuse(s2, 4, 1)

    for load in loads[2:]:
        load.wait()

    def to_modes(fields):
        both = [jnp.concatenate([g[i, 0], g[i, 1]], axis=0) for i in fields]
        along_x = left(fx, jnp.concatenate(both, axis=1))
        half_rows = n // 2
        wide = jnp.concatenate(
            [
                jnp.concatenate(
                    [along_x[:half_rows, k * n : (k + 1) * n], along_x[half_rows:, k * n : (k + 1) * n]],
                    axis=1,
                )
                for k in range(2 * len(fields))
            ],
            axis=0,
        )
        modes = right(wide, fy)
        return [modes[k * half_rows : (k + 1) * half_rows] for k in range(2 * len(fields))]

    part = n // 2 // spaces
    for j in range(2):
        for r in chunks:
            for s in range(2):
                at_s = slice(s * n, (s + 1) * n)
                g[3, j, r : r + ROWS, at_s] = rows(s2, s, 2 * j, r=r) + rows(s2, s, 2 * j + 1, r=r)
    ends_modes = to_modes([3])
    for s in range(2):
        c2out[s] = ends_modes[s]
    send(c2out, c2in, r_c2, nxt, has_next)
    is_first = jnp.where(tm == 0, 1.0, 0.0)
    for i in range(2):
        for j in range(2):
            z = 2 * j + 1
            for r in chunks:
                w = 0.0
                both = [0.0, 0.0]
                keep = [0.0, 0.0]
                for k in (z, z + 1):
                    p0 = [rows(u, 0, s, k, r=r) for s in range(2)]
                    p1 = [rows(s1, s, k, r=r) for s in range(2)]
                    p2 = [rows(s2, s, k - 1, r=r) for s in range(2)]
                    three = (p0, p1, p2)
                    w = w + sum((DT * S[i][t]) * react(*three[t]) for t in range(3))
                    for s in range(2):
                        total = sum((DT * S[i][t]) * three[t][s] for t in range(3))
                        both[s] = both[s] + total
                        if i == 0:
                            keep[s] = keep[s] + is_first * p0[s] - p1[s]
                        else:
                            keep[s] = keep[s] + p1[s] - p2[s]
                for s in range(2):
                    out_of = 0 if j == 0 else 5
                    near = 3 if j == 0 else 2
                    beyond = (DT * S[i][0]) * rows(u, 0, s, out_of, r=r) + (DT * S[i][1]) * rows(
                        s1, s, out_of, r=r
                    )
                    beyond = beyond + (
                        (DT * S[i][0]) * rows(u, 0, s, near, r=r)
                        + (DT * S[i][1]) * rows(s1, s, near, r=r)
                        + (DT * S[i][2]) * rows(s2, s, near - 1, r=r)
                    )
                    a[s, j, 8 + r : 8 + r + ROWS, :] = both[s]
                    g[i, j, r : r + ROWS, s * n : (s + 1) * n] = (
                        keep[s]
                        + SIGN[s] * w
                        - DECAY[s] * both[s]
                        + DIFFUSE[s] * (beyond - 5.0 * both[s])
                    )
            for r in chunks:
                for s in range(2):
                    around, _ = sides(s, j, r)
                    at_s = slice(s * n, (s + 1) * n)
                    g[i, j, r : r + ROWS, at_s] = (
                        g[i, j, r : r + ROWS, at_s] + DIFFUSE[s] * around
                    )
    for j in range(2):
        for r in chunks:
            for s in range(2):
                at_s = slice(s * n, (s + 1) * n)
                g[2, j, r : r + ROWS, at_s] = DIFFUSE[s] * rows(s2, s, 3 * j, r=r)

    others = to_modes([1, 2, 0])
    for i in range(3):
        for s in range(2):
            spec[s, :, i] = others[2 * i + s].reshape(spaces, part, n)
    waits_for(0, above_far)

    def exchange(k, fields):
        for d in yc:
            y, c = owner(d)
            send(
                spec.at[c, y, fields], gather.at[core, sp, fields], r_in.at[k, core, sp],
                (chip * 2 + c, y),
            )

    pl.when(has_prior)(lambda: arrived(c2in, r_c2))
    for s in range(2):
        spec[s, :, 2] = spec[s, :, 2] + c2in[s].reshape(spaces, part, n)
    exchange(0, pl.ds(0, 3))
    gather[core, sp] = spec[core, sp]
    for k, fields in ((0, pl.ds(0, 3)),):
        for d in yc:
            y, c = owner(d)
            arrived(gather.at[c, y, fields], r_in.at[k, c, y])

    m = n // 2
    power = pw[...]
    square = power * power
    columns = []
    for c in range(2):
        own = [gather[c, :, i].reshape(m, n) for i in range(3)]
        for i, field in ((0, own[2]), (1, own[0])):
            columns.append(jnp.concatenate([field, (DT * S[i][2]) * own[1]], axis=0))
    modes = left(mz, jnp.concatenate(columns, axis=1))
    d0 = [modes[:, 2 * c * n : (2 * c + 1) * n] for c in range(2)]
    d1 = [modes[:, (2 * c + 1) * n : (2 * c + 2) * n] for c in range(2)]
    e = [power * (power * d0[c] + d1[c]) for c in range(2)]
    e2[...] = square * e[0] + e[1]

    waits_for(1, chips_x - 1 - cx)
    for x in x_peers:
        send(e2, xin.at[cx], r_x.at[cx], (at(cz, x, core), sp))
    xin[cx] = e2[...]
    p4 = square * square
    p16 = p4
    for _ in range(chips_x - 1):
        p16 = p16 * p4
    for x in x_peers:
        arrived(xin.at[x], r_x.at[x])

    def add_chip(x, carry):
        running, ahead = carry
        return p4 * running + xin[x], p4 * ahead

    start = (jnp.zeros((m, n), jnp.float32), jnp.ones((m, n), jnp.float32))
    before, ahead = lax.fori_loop(0, cx, add_chip, start)
    total, _ = lax.fori_loop(cx, chips_x, add_chip, (before, ahead))
    waits_for(2, z_last - z_first)

    later = [(cz + d, at(jnp.minimum(cz + d, chips_z - 1), cx, core)) for d in range(1, half + 1)]

    @pl.when(~ends)
    def _():
        tot[...] = total

    for z, t in later[:-1]:
        send(tot, zin.at[cz - half_at], r_z.at[cz - half_at], (t, sp), ~ends & (z < z_last))

    @pl.when(half_at == 0)
    def _():
        zin[half] = jnp.zeros((m, n), jnp.float32)

    pl.when(half_at > 0)(lambda: arrived(zin.at[half], r_z.at[half]))

    def add_group(z, earlier):
        arrived(zin.at[z], r_z.at[z])
        return p16 * earlier + zin[z]

    earlier = lax.fori_loop(0, cz - half_at, add_group, zin[half])

    @pl.when(ends)
    def _():
        tot[...] = p16 * earlier + total

    for z, t in later:
        send(tot, zin.at[half], r_z.at[half], (t, sp), ends & (z < z_last))

    change = ahead * earlier + before
    changes = []
    for c in range(2):
        for source in (d0[c], d1[c]):
            change = power * (change + source)
            changes.append(change)
    at_planes = left(nz, jnp.concatenate(changes, axis=1))
    for c in range(2):
        for f in range(2):
            piece = at_planes[:, (2 * c + f) * n : (2 * c + f + 1) * n]
            fine[c, :, f] = piece.reshape(spaces, 2 * part, n)
    started = len(sends)
    for d in yc:
        y, c = owner(d)
        send(fine.at[c, y], fin.at[core, sp], r_f.at[core, sp], (chip * 2 + c, y))
    fin[core, sp] = fine[core, sp]
    finish(0, started)
    for d in yc:
        y, c = owner(d)
        arrived(fin.at[c, y], r_f.at[c, y])

    received = [fin[s, :, f].reshape(n, n) for f in range(2) for s in range(2)]
    wide = right(jnp.concatenate(received, axis=0), vy)
    for f in range(2):
        tall = []
        for s in range(2):
            rows_of = wide[(2 * f + s) * n : (2 * f + s + 1) * n]
            tall.append(jnp.concatenate([rows_of[:, :n], rows_of[:, n:]], axis=0))
        refined = left(vx, jnp.concatenate(tall, axis=1))
        for s in range(2):
            for z in range(4):
                piece = refined[z * n : (z + 1) * n, s * n : (s + 1) * n]
                swept = s1[s, z + 1] if f == 0 else s2[s, z]
                out[0, f, s, z] = swept + piece

    finish(started)


def local(shape, nodes, initial):
    count, spaces, chips_x, chips_z, n = shape
    consts = tables(n, spaces)
    m = n // 2
    part = m // spaces
    f32 = jnp.float32
    vmem, sem = pltpu.VMEM, pltpu.SemaphoreType.DMA
    n_sends = 4 + 1 + 4 + 2 + 1 + 3 * (2 * spaces - 1) + chips_x - 1 + chips_z - 1
    scratch = [
        vmem((3, 2, 6, n, n), f32),
        vmem((2, 6, n, n), f32),
        vmem((2, 4, n, n), f32),
        vmem((2, 6, n + 16, n), f32),
        vmem((4, 2, n, 2 * n), f32),
    ]
    scratch += [vmem(c.shape, jnp.bfloat16) for c in consts[:-1]]
    scratch += [
        vmem((m, n), f32),
        vmem((2, 2, n, n), f32),
        vmem((2, 2, n, n), f32),
        vmem((2, spaces, 3, part, n), f32),
        vmem((2, m, n), f32),
        vmem((2, m, n), f32),
        vmem((2, spaces, 3, part, n), f32),
        vmem((m, n), f32),
        vmem((chips_x, m, n), f32),
        vmem((m, n), f32),
        vmem((chips_z // 2 + 1, m, n), f32),
        vmem((2, spaces, 2, 2 * part, n), f32),
        vmem((2, spaces, 2, 2 * part, n), f32),
        sem((n_sends,)),
        sem((9,)),
        sem(()),
        sem((2, 2)),
        sem((2,)),
        sem((2,)),
        sem(()),
        sem((2, 2, spaces)),
        sem((chips_x,)),
        sem((chips_z // 2 + 1,)),
        sem((2, spaces)),
        pltpu.SemaphoreType.REGULAR((3,)),
    ]
    operands = [nodes, initial, *[jnp.asarray(c) for c in consts]]
    anywhere = pl.BlockSpec(memory_space=pl.ANY)
    return pl.pallas_call(
        functools.partial(kernel, shape),
        out_shape=jax.ShapeDtypeStruct((1, 2, 2, 4, n, n), f32),
        in_specs=[anywhere] * (2 + len(consts)),
        out_specs=pl.BlockSpec(memory_space=pltpu.VMEM),
        scratch_shapes=scratch,
        compiler_params=pltpu.CompilerParams(
            collective_id=0, has_side_effects=True, vmem_limit_bytes=40 << 20
        ),
        name="iteration",
    )(*[pltpu.with_memory_space_constraint(x, pltpu.HBM) for x in operands])


def solution(mesh):
    count, spaces = mesh.shape["tm"], mesh.shape["space"]
    chips_x = 4 if count == 64 else 2
    chips_z = count // (2 * chips_x)
    in_specs = (P("tm", None, None, "space", None, None), P(None, "space", None, None))
    out_specs = P("tm", None, None, "space", None, None)

    def run(nodes, initial):
        shape = (count, spaces, chips_x, chips_z, nodes.shape[-1])
        return jax.shard_map(
            functools.partial(local, shape),
            mesh=mesh, in_specs=in_specs, out_specs=out_specs, check_vma=False,
        )(nodes, initial)

    return run
```

```python
import functools
import math

import jax
import jax.numpy as jnp
import ml_dtypes
import numpy as np
from jax import lax
from jax.experimental import pallas as pl
from jax.experimental.pallas import tpu as pltpu
from jax.sharding import PartitionSpec as P

MESH = pl.DeviceIdType.MESH
DIFFUSE = (0.5, 0.25)
DECAY = (0.04, 0.1)
SIGN = (-1.0, 1.0)
DT = 0.5
H = 0.25
S = ((5.0 / 24.0, 1.0 / 3.0, -1.0 / 24.0), (-1.0 / 24.0, 1.0 / 3.0, 5.0 / 24.0))
ROWS = 16


def sine_table(points, modes, stretch):
    place = np.arange(points) + 0.5
    order = np.arange(modes) + 1.0
    angle = math.pi / (stretch * modes) * place[:, None] * order[None, :]
    weight = np.where(np.arange(modes) == modes - 1, math.sqrt(0.5), 1.0)
    return math.sqrt(2.0 / modes) * weight[None, :] * np.sin(angle)


def two_parts(table):
    high = table.astype(np.float32).astype(ml_dtypes.bfloat16)
    low = (table - high.astype(np.float64)).astype(np.float32).astype(ml_dtypes.bfloat16)
    return np.stack([high, low])


@functools.lru_cache(maxsize=None)
def tables(n, spaces):
    m, mz = n // 2, 2 * spaces
    half = m // 2
    per = half // spaces
    average = np.kron(np.eye(m), np.array([[0.5, 0.5]]))
    fine = sine_table(m, m, 1.0).T @ average
    fx = np.zeros((2, half, 2, 2, n))
    for z in range(2):
        fx[:, :, z, z, :] = 0.5 * fine.reshape(2, half, n)
    fx = fx.reshape(2 * m, 2 * n)
    fy = np.kron(np.eye(2), fine.T)
    wz = sine_table(mz, mz, 1.0).T
    own = np.zeros((mz, per, spaces, per, 2))
    edge = np.zeros((mz, per, spaces, per, 2))
    for i in range(per):
        for y in range(spaces):
            for z in range(2):
                own[:, i, y, i, z] = wz[:, 2 * y + z]
            if y > 0:
                edge[:, i, y, i, 0] = wz[:, 2 * y - 1]
            if y < spaces - 1:
                edge[:, i, y, i, 1] = wz[:, 2 * y + 2]
    own, edge = own.reshape(m, m), edge.reshape(m, m)
    mats = np.concatenate([own, edge], axis=1)
    nz = np.kron(sine_table(2 * mz, mz, 2.0), np.eye(per))
    vxy = sine_table(n, m, 2.0)
    vy = np.kron(np.eye(2), vxy.T)
    vx = np.zeros((4, n, 2, spaces, 4, per))
    for f in range(4):
        vx[f, :, :, :, f, :] = vxy.reshape(n, 2, spaces, per)
    vx = vx.reshape(4 * n, 2 * spaces * 4 * per)

    def eigen(modes):
        return 2.0 * np.cos(math.pi * (np.arange(modes) + 1.0) / modes) - 2.0

    ab = (eigen(m)[:, None] + eigen(m)[None, :]).reshape(2, spaces, per, m)
    e = (eigen(mz)[None, :, None, None, None] + ab.transpose(1, 2, 0, 3)[:, None]) / 4.0
    lin = np.stack([d * e - k for d, k in zip(DIFFUSE, DECAY)])
    factor = 1.0 / (1.0 - H * lin)
    factor = factor.reshape(2, spaces, m, n).astype(np.float32)
    return tuple(map(two_parts, (fx, fy, mats, nz, vy, vx))) + (factor,)


def split(x):
    high = x.astype(jnp.bfloat16)
    low = (x - high.astype(jnp.float32)).astype(jnp.bfloat16)
    return high, low


def dot(a, b):
    return jnp.dot(a, b, preferred_element_type=jnp.float32)


def left(table, x):
    high, low = split(x)
    return dot(table[0], high) + (dot(table[0], low) + dot(table[1], high))


def right(x, table):
    high, low = split(x)
    return dot(high, table[0]) + (dot(low, table[0]) + dot(high, table[1]))


def kernel(
    shape,
    nodes, initial, fx_h, fy_h, mz_h, nz_h, vy_h, vx_h, p_h,
    out,
    u, s1, s2, a, g, fx, fy, mz, nz, vy, vx, pw,
    sx, rim, spec, c2out, c2in, gather, e2, xin, tot, zin, fine, fin,
    ssem, lsem, r_u0, r_h, r_u0h, r_s1, r_c2, r_in, r_x, r_z, r_f, credit,
):
    count, spaces, chips_x, chips_z, n = shape
    tm, sp = lax.axis_index("tm"), lax.axis_index("space")
    core = lax.rem(tm, 2)
    chip = tm // 2
    cx, cz = lax.rem(chip, chips_x), chip // chips_x
    sends = []

    def at(z, x, c):
        return (z * chips_x + x) * 2 + c

    def send(src, dst, sem, device, when=None):
        copy = pltpu.make_async_remote_copy(
            src, dst, ssem.at[len(sends)], sem, device_id=device, device_id_type=MESH
        )
        sends.append((copy, when))
        if when is None:
            copy.start()
        else:
            pl.when(when)(copy.start)

    def finish(first, last=None):
        for copy, when in sends[first:last]:
            if when is None:
                copy.wait_send()
            else:
                pl.when(when)(copy.wait_send)

    def arrived(dst, sem):
        pltpu.make_async_copy(dst, dst, sem).wait()

    has_lo, has_hi = sp > 0, sp < spaces - 1
    lo, hi = (tm, jnp.maximum(sp - 1, 0)), (tm, jnp.minimum(sp + 1, spaces - 1))
    has_next, has_prior = tm < count - 1, tm > 0
    nxt = (lax.rem(tm + 1, count), sp)
    prv = (lax.rem(tm + count - 1, count), sp)
    ring = sorted(range(spaces), key=lambda d: -min(d, spaces - d))
    yc = [(d, c) for d in ring for c in (1, 0) if (d, c) != (0, 0)]

    def owner(d):
        return lax.rem(sp + d[0], spaces), lax.rem(core + d[1], 2)

    x_peers = [lax.rem(cx + d, chips_x) for d in (2, 1, 3) if d < chips_x]
    if chips_x == 2:
        x_peers = [1 - cx]

    loads = [
        pltpu.make_async_copy(nodes.at[0, 0], u.at[1, :, pl.ds(1, 4)], lsem.at[0]),
        pltpu.make_async_copy(nodes.at[0, 1], u.at[2, :, pl.ds(1, 4)], lsem.at[1]),
        pltpu.make_async_copy(fx_h, fx, lsem.at[2]),
        pltpu.make_async_copy(fy_h, fy, lsem.at[3]),
        pltpu.make_async_copy(mz_h, mz, lsem.at[4]),
        pltpu.make_async_copy(nz_h, nz, lsem.at[5]),
        pltpu.make_async_copy(vy_h, vy, lsem.at[6]),
        pltpu.make_async_copy(vx_h, vx, lsem.at[7]),
        pltpu.make_async_copy(p_h.at[core, sp], pw, lsem.at[8]),
    ]
    for load in loads:
        load.start()
    whole = pl.ds(1, 4)

    @pl.when(tm == 0)
    def _():
        pltpu.make_async_copy(initial, u.at[0, :, whole], r_u0).start()

    barrier = pltpu.get_barrier_semaphore()

    def one(flag):
        return jnp.where(flag, 1, 0)

    sibling = tm + 1 - 2 * core
    beside = lax.rem(tm + count - 1 + 2 * core, count)
    has_beside = jnp.where(core == 1, has_next, has_prior)

    half = chips_z // 2
    half_at = (cz // half) * half
    ends = cz == half_at + half - 1
    z_first = cz + 1
    z_last = jnp.where(ends, jnp.minimum(half_at + 2 * half, chips_z), half_at + half)
    z_below = cz - half_at + one(half_at > 0)

    def greet(t, y):
        pl.semaphore_signal(barrier, 1, device_id=(t, y), device_id_type=MESH)

    def answer(which, t, y):
        pl.semaphore_signal(credit.at[which], 1, device_id=(t, y), device_id_type=MESH)

    def waits_for(which, answers):
        pl.when(answers > 0)(lambda: pl.semaphore_wait(credit.at[which], answers))

    def over(lower, upper, work):
        def step(i, carry):
            work(i)
            return carry

        lax.fori_loop(lower, upper, step, 0)

    def far_columns(y, call):
        call(sibling, y)
        pl.when((y != sp + 1) & (y != sp - 1))(lambda: call(tm, y))

    pl.when(has_hi)(lambda: greet(tm, hi[1]))
    pl.when(has_lo)(lambda: greet(tm, lo[1]))
    greet(sibling, sp)
    pl.when(has_beside)(lambda: greet(beside, sp))
    over(sp + 1, spaces, lambda y: far_columns(y, greet))
    over(cx + 1, chips_x, lambda x: greet(at(cz, x, core), sp))
    over(z_first, z_last, lambda z: greet(at(z, cx, core), sp))

    below_far = 2 * sp - one(has_lo)
    above_far = 2 * (spaces - 1 - sp) - one(has_hi)
    pl.semaphore_wait(
        barrier,
        one(has_lo) + one(has_hi) + 1 + one(has_beside)
        + below_far + cx + z_below,
    )

    send(nodes.at[0, 1], u.at[0, :, whole], r_u0, nxt, has_next)
    for node in (2, 1):
        send(nodes.at[0, node - 1, :, 3], u.at[node, :, 0], r_h.at[node - 1, 0], hi, has_hi)
        send(nodes.at[0, node - 1, :, 0], u.at[node, :, 5], r_h.at[node - 1, 1], lo, has_lo)
    over(0, sp, lambda y: far_columns(y, functools.partial(answer, 0)))
    over(0, cx, lambda x: answer(1, at(cz, x, core), sp))
    over(half_at, cz, lambda z: answer(2, at(z, cx, core), sp))
    pl.when(half_at > 0)(lambda: answer(2, at(half_at - 1, cx, core), sp))

    zero = jnp.zeros((n, n), jnp.float32)
    for s in range(2):
        for z in range(6):
            a[s, z, 0:8, :] = jnp.zeros((8, n), jnp.float32)
            a[s, z, 8 + n : 16 + n, :] = jnp.zeros((8, n), jnp.float32)

    def outside(plane):
        for s in range(2):
            for i in range(3):
                u[i, s, plane] = zero
            s1[s, plane] = zero

    pl.when(sp == 0)(lambda: outside(0))
    pl.when(sp == spaces - 1)(lambda: outside(5))

    @pl.when(tm == 0)
    def _():
        c2in[...] = jnp.zeros(c2in.shape, jnp.float32)

    lane = lax.broadcasted_iota(jnp.int32, (ROWS, n), 1)
    first_lane, last_lane = lane == 0, lane == n - 1
    chunks = range(0, n, ROWS)

    def react(p, q):
        return (1.0 + p) * (q * q)

    def sides(s, z, r):
        mid = a[s, z, 8 + r : 8 + r + ROWS, :]
        west = jnp.where(first_lane, 0.0, pltpu.roll(mid, 1, 1))
        east = jnp.where(last_lane, 0.0, pltpu.roll(mid, n - 1, 1))
        north = a[s, z, 7 + r : 7 + r + ROWS, :]
        south = a[s, z, 9 + r : 9 + r + ROWS, :]
        return (west + east) + (north + south), mid

    def rows(ref, *index, r):
        return ref[(*index, slice(r, r + ROWS), slice(None))]

    def sum_one(z, base=True):
        for r in chunks:
            pq = [[rows(u, i, s, z, r=r) for s in range(2)] for i in range(3)]
            if base:
                w = sum((DT * S[0][i]) * react(*pq[i]) for i in range(3))
            for s in range(2):
                total = sum((DT * S[0][i]) * pq[i][s] for i in range(3))
                a[s, z, 8 + r : 8 + r + ROWS, :] = total
                if base:
                    s1[s, z, r : r + ROWS, :] = pq[0][s] + SIGN[s] * w - DECAY[s] * total

    def begin_one(z):
        for r in chunks:
            pq = [[rows(u, i, s, z, r=r) for s in range(2)] for i in (1, 2)]
            w = sum((DT * S[0][i + 1]) * react(*pq[i]) for i in range(2))
            for s in range(2):
                total = sum((DT * S[0][i + 1]) * pq[i][s] for i in range(2))
                a[s, z, 8 + r : 8 + r + ROWS, :] = total
                s1[s, z, r : r + ROWS, :] = SIGN[s] * w - DECAY[s] * total

    def end_one(z):
        weight = DT * S[0][0]
        for r in chunks:
            pq = [rows(u, 0, s, z, r=r) for s in range(2)]
            w = weight * react(*pq)
            for s in range(2):
                own = weight * pq[s]
                at_r = slice(8 + r, 8 + r + ROWS)
                a[s, z, at_r, :] = a[s, z, at_r, :] + own
                s1[s, z, r : r + ROWS, :] = rows(s1, s, z, r=r) + (
                    pq[s] + SIGN[s] * w - DECAY[s] * own
                )

    def sum_two(z, base=True):
        weight = (DT * S[1][0], DT * S[1][1] - H, DT * S[1][2])
        for r in chunks:
            pq = [[rows(u, i, s, z, r=r) for s in range(2)] for i in range(3)]
            ab = [rows(s1, s, z, r=r) for s in range(2)]
            if base:
                w = H * react(*ab) + sum(weight[i] * react(*pq[i]) for i in range(3))
            for s in range(2):
                total = H * ab[s] + sum(weight[i] * pq[i][s] for i in range(3))
                a[s, z, 8 + r : 8 + r + ROWS, :] = total
                if base:
                    s2[s, z - 1, r : r + ROWS, :] = ab[s] + SIGN[s] * w - DECAY[s] * total

    def diffuse(ref, z, shift):
        for r in chunks:
            for s in range(2):
                around, mid = sides(s, z, r)
                below = a[s, z - 1, 8 + r : 8 + r + ROWS, :]
                above = a[s, z + 1, 8 + r : 8 + r + ROWS, :]
                lap = around + (below + above) - 6.0 * mid
                ref[s, z - shift, r : r + ROWS, :] = (
                    ref[s, z - shift, r : r + ROWS, :] + DIFFUSE[s] * lap
                )

    loads[0].wait()
    loads[1].wait()
    for z in (1, 2, 3, 4):
        begin_one(z)
    pl.when(has_lo)(lambda: arrived(u.at[2, :, 0], r_h.at[1, 0]))
    pl.when(has_hi)(lambda: arrived(u.at[2, :, 5], r_h.at[1, 1]))
    send(u.at[2, :, 0], u.at[0, :, 0], r_u0h.at[0], nxt, has_lo & has_next)
    send(u.at[2, :, 5], u.at[0, :, 5], r_u0h.at[1], nxt, has_hi & has_next)
    arrived(u.at[0, :, whole], r_u0)
    send(u.at[0, :, 4], u.at[0, :, 0], r_u0h.at[0], hi, has_hi & ~has_prior)
    send(u.at[0, :, 1], u.at[0, :, 5], r_u0h.at[1], lo, has_lo & ~has_prior)
    for z in (1, 2, 3, 4):
        end_one(z)
    edges = ((0, 1, 2, 0), (1, 4, 3, 5))
    for k, z, inner, _ in edges:
        for r in chunks:
            for s in range(2):
                around, mid = sides(s, z, r)
                lap = around + a[s, inner, 8 + r : 8 + r + ROWS, :] - 6.0 * mid
                sx[k, s, r : r + ROWS, :] = rows(s1, s, z, r=r) + DIFFUSE[s] * lap
                rim[k, s, r : r + ROWS, :] = DIFFUSE[s] * mid
        if k == 0:
            send(sx.at[0], s1.at[:, 5], r_s1.at[1], lo, has_lo)
        else:
            send(sx.at[1], s1.at[:, 0], r_s1.at[0], hi, has_hi)
    for z in (2, 3):
        diffuse(s1, z, 0)
    for k, z, _, outer in edges:
        has = (has_lo, has_hi)[k]
        ready = [(u.at[1, :, outer], r_h.at[0, k]), (u.at[0, :, outer], r_u0h.at[k])]
        for dst, landed in ready:
            pl.when(has)(functools.partial(arrived, dst, landed))
        sum_one(outer, False)
        for r in chunks:
            for s in range(2):
                beyond = a[s, outer, 8 + r : 8 + r + ROWS, :]
                s1[s, z, r : r + ROWS, :] = sx[k, s, r : r + ROWS, :] + DIFFUSE[s] * beyond

    for z in (1, 2, 3, 4):
        sum_two(z)
    for z in (2, 3):
        diffuse(s2, z, 1)

    def complete(k, outer):
        arrived(s1.at[:, outer], r_s1.at[k])
        for r in chunks:
            for s in range(2):
                s1[s, outer, r : r + ROWS, :] = rows(s1, s, outer, r=r) + rim[k, s, r : r + ROWS, :]

    pl.when(has_lo)(lambda: complete(0, 0))
    sum_two(0, False)
    pl.when(has_hi)(lambda: complete(1, 5))
    sum_two(5, False)
    diffuse(s2, 1, 1)
    diffuse(s2, 4, 1)

    for load in loads[2:]:
        load.wait()

    def to_modes(fields):
        both = [jnp.concatenate([g[i, 0], g[i, 1]], axis=0) for i in fields]
        along_x = left(fx, jnp.concatenate(both, axis=1))
        half_rows = n // 2
        wide = jnp.concatenate(
            [
                jnp.concatenate(
                    [along_x[:half_rows, k * n : (k + 1) * n], along_x[half_rows:, k * n : (k + 1) * n]],
                    axis=1,
                )
                for k in range(2 * len(fields))
            ],
            axis=0,
        )
        modes = right(wide, fy)
        return [modes[k * half_rows : (k + 1) * half_rows] for k in range(2 * len(fields))]

    part = n // 2 // spaces
    for j in range(2):
        for r in chunks:
            for s in range(2):
                at_s = slice(s * n, (s + 1) * n)
                g[3, j, r : r + ROWS, at_s] = rows(s2, s, 2 * j, r=r) + rows(s2, s, 2 * j + 1, r=r)
    ends_modes = to_modes([3])
    for s in range(2):
        c2out[s] = ends_modes[s]
    send(c2out, c2in, r_c2, nxt, has_next)
    is_first = jnp.where(tm == 0, 1.0, 0.0)
    for i in range(2):
        for j in range(2):
            z = 2 * j + 1
            for r in chunks:
                w = 0.0
                both = [0.0, 0.0]
                keep = [0.0, 0.0]
                for k in (z, z + 1):
                    p0 = [rows(u, 0, s, k, r=r) for s in range(2)]
                    p1 = [rows(s1, s, k, r=r) for s in range(2)]
                    p2 = [rows(s2, s, k - 1, r=r) for s in range(2)]
                    three = (p0, p1, p2)
                    w = w + sum((DT * S[i][t]) * react(*three[t]) for t in range(3))
                    for s in range(2):
                        total = sum((DT * S[i][t]) * three[t][s] for t in range(3))
                        both[s] = both[s] + total
                        if i == 0:
                            keep[s] = keep[s] + is_first * p0[s] - p1[s]
                        else:
                            keep[s] = keep[s] + p1[s] - p2[s]
                for s in range(2):
                    out_of = 0 if j == 0 else 5
                    near = 3 if j == 0 else 2
                    beyond = (DT * S[i][0]) * rows(u, 0, s, out_of, r=r) + (DT * S[i][1]) * rows(
                        s1, s, out_of, r=r
                    )
                    beyond = beyond + (
                        (DT * S[i][0]) * rows(u, 0, s, near, r=r)
                        + (DT * S[i][1]) * rows(s1, s, near, r=r)
                        + (DT * S[i][2]) * rows(s2, s, near - 1, r=r)
                    )
                    a[s, j, 8 + r : 8 + r + ROWS, :] = both[s]
                    g[i, j, r : r + ROWS, s * n : (s + 1) * n] = (
                        keep[s]
                        + SIGN[s] * w
                        - DECAY[s] * both[s]
                        + DIFFUSE[s] * (beyond - 5.0 * both[s])
                    )
            for r in chunks:
                for s in range(2):
                    around, _ = sides(s, j, r)
                    at_s = slice(s * n, (s + 1) * n)
                    g[i, j, r : r + ROWS, at_s] = (
                        g[i, j, r : r + ROWS, at_s] + DIFFUSE[s] * around
                    )
    for j in range(2):
        for r in chunks:
            for s in range(2):
                at_s = slice(s * n, (s + 1) * n)
                g[2, j, r : r + ROWS, at_s] = DIFFUSE[s] * rows(s2, s, 3 * j, r=r)

    others = to_modes([1, 2, 0])
    for i in range(3):
        for s in range(2):
            spec[s, :, i] = others[2 * i + s].reshape(spaces, part, n)
    waits_for(0, above_far)

    def exchange(k, fields):
        for d in yc:
            y, c = owner(d)
            send(
                spec.at[c, y, fields], gather.at[core, sp, fields], r_in.at[k, core, sp],
                (chip * 2 + c, y),
            )

    pl.when(has_prior)(lambda: arrived(c2in, r_c2))
    for s in range(2):
        spec[s, :, 2] = spec[s, :, 2] + c2in[s].reshape(spaces, part, n)
    exchange(0, pl.ds(0, 3))
    gather[core, sp] = spec[core, sp]
    for k, fields in ((0, pl.ds(0, 3)),):
        for d in yc:
            y, c = owner(d)
            arrived(gather.at[c, y, fields], r_in.at[k, c, y])

    m = n // 2
    power = pw[...]
    square = power * power
    columns = []
    for c in range(2):
        own = [gather[c, :, i].reshape(m, n) for i in range(3)]
        for i, field in ((0, own[2]), (1, own[0])):
            columns.append(jnp.concatenate([field, (DT * S[i][2]) * own[1]], axis=0))
    modes = left(mz, jnp.concatenate(columns, axis=1))
    d0 = [modes[:, 2 * c * n : (2 * c + 1) * n] for c in range(2)]
    d1 = [modes[:, (2 * c + 1) * n : (2 * c + 2) * n] for c in range(2)]
    e = [power * (power * d0[c] + d1[c]) for c in range(2)]
    e2[...] = square * e[0] + e[1]

    waits_for(1, chips_x - 1 - cx)
    for x in x_peers:
        send(e2, xin.at[cx], r_x.at[cx], (at(cz, x, core), sp))
    xin[cx] = e2[...]
    p4 = square * square
    p16 = p4
    for _ in range(chips_x - 1):
        p16 = p16 * p4
    for x in x_peers:
        arrived(xin.at[x], r_x.at[x])

    def add_chip(x, carry):
        running, ahead = carry
        return p4 * running + xin[x], p4 * ahead

    start = (jnp.zeros((m, n), jnp.float32), jnp.ones((m, n), jnp.float32))
    before, ahead = lax.fori_loop(0, cx, add_chip, start)
    total, _ = lax.fori_loop(cx, chips_x, add_chip, (before, ahead))
    waits_for(2, z_last - z_first)

    later = [(cz + d, at(jnp.minimum(cz + d, chips_z - 1), cx, core)) for d in range(1, half + 1)]

    @pl.when(~ends)
    def _():
        tot[...] = total

    for z, t in later[:-1]:
        send(tot, zin.at[cz - half_at], r_z.at[cz - half_at], (t, sp), ~ends & (z < z_last))

    @pl.when(half_at == 0)
    def _():
        zin[half] = jnp.zeros((m, n), jnp.float32)

    pl.when(half_at > 0)(lambda: arrived(zin.at[half], r_z.at[half]))

    def add_group(z, earlier):
        arrived(zin.at[z], r_z.at[z])
        return p16 * earlier + zin[z]

    earlier = lax.fori_loop(0, cz - half_at, add_group, zin[half])

    @pl.when(ends)
    def _():
        tot[...] = p16 * earlier + total

    for z, t in later:
        send(tot, zin.at[half], r_z.at[half], (t, sp), ends & (z < z_last))

    change = ahead * earlier + before
    changes = []
    for c in range(2):
        for source in (d0[c], d1[c]):
            change = power * (change + source)
            changes.append(change)
    at_planes = left(nz, jnp.concatenate(changes, axis=1))
    for c in range(2):
        for f in range(2):
            piece = at_planes[:, (2 * c + f) * n : (2 * c + f + 1) * n]
            fine[c, :, f] = piece.reshape(spaces, 2 * part, n)
    started = len(sends)
    for d in yc:
        y, c = owner(d)
        send(fine.at[c, y], fin.at[core, sp], r_f.at[core, sp], (chip * 2 + c, y))
    fin[core, sp] = fine[core, sp]
    finish(0, started)
    for d in yc:
        y, c = owner(d)
        arrived(fin.at[c, y], r_f.at[c, y])

    received = [fin[s, :, f].reshape(n, n) for f in range(2) for s in range(2)]
    wide = right(jnp.concatenate(received, axis=0), vy)
    for f in range(2):
        tall = []
        for s in range(2):
            rows_of = wide[(2 * f + s) * n : (2 * f + s + 1) * n]
            tall.append(jnp.concatenate([rows_of[:, :n], rows_of[:, n:]], axis=0))
        refined = left(vx, jnp.concatenate(tall, axis=1))
        for s in range(2):
            for z in range(4):
                piece = refined[z * n : (z + 1) * n, s * n : (s + 1) * n]
                swept = s1[s, z + 1] if f == 0 else s2[s, z]
                out[0, f, s, z] = swept + piece

    finish(started)


def local(shape, nodes, initial):
    count, spaces, chips_x, chips_z, n = shape
    consts = tables(n, spaces)
    m = n // 2
    part = m // spaces
    f32 = jnp.float32
    vmem, sem = pltpu.VMEM, pltpu.SemaphoreType.DMA
    n_sends = 4 + 1 + 4 + 2 + 1 + 3 * (2 * spaces - 1) + chips_x - 1 + chips_z - 1
    scratch = [
        vmem((3, 2, 6, n, n), f32),
        vmem((2, 6, n, n), f32),
        vmem((2, 4, n, n), f32),
        vmem((2, 6, n + 16, n), f32),
        vmem((4, 2, n, 2 * n), f32),
    ]
    scratch += [vmem(c.shape, jnp.bfloat16) for c in consts[:-1]]
    scratch += [
        vmem((m, n), f32),
        vmem((2, 2, n, n), f32),
        vmem((2, 2, n, n), f32),
        vmem((2, spaces, 3, part, n), f32),
        vmem((2, m, n), f32),
        vmem((2, m, n), f32),
        vmem((2, spaces, 3, part, n), f32),
        vmem((m, n), f32),
        vmem((chips_x, m, n), f32),
        vmem((m, n), f32),
        vmem((chips_z // 2 + 1, m, n), f32),
        vmem((2, spaces, 2, 2 * part, n), f32),
        vmem((2, spaces, 2, 2 * part, n), f32),
        sem((n_sends,)),
        sem((9,)),
        sem(()),
        sem((2, 2)),
        sem((2,)),
        sem((2,)),
        sem(()),
        sem((2, 2, spaces)),
        sem((chips_x,)),
        sem((chips_z // 2 + 1,)),
        sem((2, spaces)),
        pltpu.SemaphoreType.REGULAR((3,)),
    ]
    operands = [nodes, initial, *[jnp.asarray(c) for c in consts]]
    anywhere = pl.BlockSpec(memory_space=pl.ANY)
    return pl.pallas_call(
        functools.partial(kernel, shape),
        out_shape=jax.ShapeDtypeStruct((1, 2, 2, 4, n, n), f32),
        in_specs=[anywhere] * (2 + len(consts)),
        out_specs=pl.BlockSpec(memory_space=pltpu.VMEM),
        scratch_shapes=scratch,
        compiler_params=pltpu.CompilerParams(
            collective_id=0, has_side_effects=True, vmem_limit_bytes=40 << 20
        ),
        name="iteration",
    )(*[pltpu.with_memory_space_constraint(x, pltpu.HBM) for x in operands])


def solution(mesh):
    count, spaces = mesh.shape["tm"], mesh.shape["space"]
    chips_x = 4 if count == 64 else 2
    chips_z = count // (2 * chips_x)
    in_specs = (P("tm", None, None, "space", None, None), P(None, "space", None, None))
    out_specs = P("tm", None, None, "space", None, None)

    def run(nodes, initial):
        shape = (count, spaces, chips_x, chips_z, nodes.shape[-1])
        return jax.shard_map(
            functools.partial(local, shape),
            mesh=mesh, in_specs=in_specs, out_specs=out_specs, check_vma=False,
        )(nodes, initial)

    return run
```
